256 devices in a mesh: fsdp: 64 (over z, x, core), rep: 4 (over y).
Axes of the slice: x: 4, y: 4, z: 8, core: 2. Of those that a mesh axis runs over, the one named last changes fastest.
Arguments:
- acts: bfloat16 [262144, 1536], P(('fsdp', 'rep')), may hold values from -24 to 24
- cotangent: bfloat16 [262144, 4096], P(('fsdp', 'rep')), may hold values from -0.01171875 to 0.01171875
- master: float32 [1536, 4096], P(('fsdp', 'rep')), may hold values from -6 to 6
- moment: float32 [1536, 4096], P(('fsdp', 'rep')), may hold values from -4 to 4
- second: float32 [1536, 4096], P(('fsdp', 'rep')), may hold values from 0.01 to 2
Outputs:
- new_master: float32 [1536, 4096], P(('fsdp', 'rep'))
- new_moment: float32 [1536, 4096], P(('fsdp', 'rep'))
- new_second: float32 [1536, 4096], P(('fsdp', 'rep'))
- params: bfloat16 [1536, 4096], P('fsdp')
The draws below stay inside these ranges and needn't reach their ends.
All inputs are finite; a program needn't handle non-finite values.
Results may differ from the reference program's by a relative error of at most 0.0049.
Values may be sent and summed in bfloat16 or wider, within the bound.
No kernel may reach another device: no remote copies, remote signals or barrier semaphores. Data moves between devices by JAX's collectives and lax.ppermute only.
A program may use at most 128 MiB of HBM per device.

```python
import math
import jax
import jax.numpy as jnp
from jax import lax

D = 1536
FFW = 4096
TOKENS = 262144


def with_spikes(values, own_key, source, target, parts, factor):
    owner, partner = [(jnp.arange(values.shape[dim]) // (values.shape[dim] // parts)).reshape([-1 if axis == dim else 1 for axis in range(values.ndim)]) for dim in (source, target)]
    chosen = jax.random.permutation(own_key, parts)[partner]
    strong = (owner == chosen) | (owner == (partner + parts // 2) % parts)
    return jnp.where(strong, factor * values, values)


def level_of(own_key, dims, pieces, least, high):
    level = 1.0
    for dim, shards_of in pieces:
        heights = jax.random.uniform(jax.random.fold_in(jax.random.fold_in(own_key, 6), dim), (shards_of,), jnp.float32, least / len(pieces), high / len(pieces))
        level = level * jnp.repeat(jnp.exp(heights), dims[dim] // shards_of).reshape((-1,) + (1,) * (len(dims) - 1 - dim))
    return level


def normal_values(stream_key, dims, width, reach, cuts=(), held_as=jnp.bfloat16):
    entries = width * jax.random.normal(stream_key, dims, jnp.float32)
    if cuts:
        entries = entries * level_of(stream_key, dims, cuts, -0.22, 0.18)
    return jnp.clip(entries, -reach, reach).astype(held_as)


def bell_draw_with(key, extent, spread, bound, cuts, heavy, held_as=jnp.bfloat16):
    entries = spread * jax.random.normal(key, extent, jnp.float32)
    if cuts:
        entries = entries * level_of(key, extent, cuts, -0.22, 0.18)
    return jnp.clip(with_spikes(entries, jax.random.fold_in(key, 3), *heavy), -bound, bound).astype(held_as)


def setup_inputs(seed: int = 0) -> dict:
    streams_of = jax.random.split(jax.random.key(seed), 6)
    acts = bell_draw_with(streams_of[0], (TOKENS, D), 1.0, 24.0, ((0, 256),), (0, 1, 256, 6.0))
    cotangent = normal_values(streams_of[1], (TOKENS, FFW), TOKENS ** -0.5, 0.01171875, ((0, 256),))
    master = normal_values(streams_of[2], (D, FFW), 1.0, 6.0, ((0, 256),), jnp.float32)
    moment = normal_values(streams_of[3], (D, FFW), 0.5, 4.0, ((0, 256),), jnp.float32)
    second = jnp.clip(jnp.exp(math.log(2.0) - 5.2983174 * jax.random.uniform(streams_of[4], (D, FFW), jnp.float32) ** level_of(streams_of[4], (D, FFW), ((0, 256),), -0.2, 0.2)), 0.01, 2.0)
    return dict(acts=acts, cotangent=cotangent, master=master, moment=moment, second=second)


def reference(acts, cotangent, master, moment, second):
    grad = lax.dot_general(acts, cotangent, (((0,), (0,)), ((), ())), preferred_element_type=jnp.float32)
    new_moment = 0.9 * moment + 0.1 * grad
    new_second = 0.95 * second + 0.05 * grad * grad
    corr_one = 1.0 - 0.9 ** 10
    corr_two = 1.0 - 0.95 ** 10
    update = new_moment / corr_one / (jnp.sqrt(new_second / corr_two) + 1e-08)
    new_master = master - 0.02 * (update + 0.1 * master)
    return (new_master, new_moment, new_second, new_master.astype(jnp.bfloat16))
```

```python
import jax
import jax.numpy as jnp
from jax import lax
from jax.experimental import pallas as pl
from jax.experimental.pallas import tpu as pltpu
from jax.sharding import Mesh, PartitionSpec as P

NZ, NX, NC, NY = 8, 4, 2, 4
D, FFW = 1536, 4096
HALF = FFW // 2
TN = 256
BLK = D // (NZ * NX)
FLOW_C = 1024
FLOW_B = 1024
T = 1024
F32, BF16 = jnp.float32, jnp.bfloat16
VMEM_LIMIT = 48 * 1024 * 1024
DN = (((0,), (0,)), ((), ()))


def params_of(flops, nbytes):
    return dict(
        compiler_params=pltpu.CompilerParams(vmem_limit_bytes=VMEM_LIMIT),
        cost_estimate=pl.CostEstimate(flops=flops, bytes_accessed=nbytes, transcendentals=0),
    )


def shift(v, axis, n, s):
    return lax.ppermute(v, axis, [(i, (i + s) % n) for i in range(n)])


def product(acts, cot, idx, base, ncols):
    def kernel(idx_ref, a, c, o):
        o[...] = lax.dot_general(a[...], c[...], DN, preferred_element_type=F32).astype(BF16)

    return pl.pallas_call(
        kernel,
        grid_spec=pltpu.PrefetchScalarGridSpec(
            num_scalar_prefetch=1,
            grid=(ncols // TN,),
            in_specs=[
                pl.BlockSpec((T, D), lambda j, s: (0, 0)),
                pl.BlockSpec((T, TN), lambda j, s: (0, (1 - s[0]) * (HALF // TN) + base // TN + j)),
            ],
            out_specs=pl.BlockSpec((D, TN), lambda j, s: (0, j)),
        ),
        out_shape=jax.ShapeDtypeStruct((D, ncols), BF16),
        name="product_theirs",
        **params_of(2 * T * D * ncols, 2 * (T * D + T * ncols + D * ncols)),
    )(idx, acts, cot)


def product_for_y(acts, cot, got, idx, base):
    def kernel(idx_ref, a, c, r, *outs):
        acc = lax.dot_general(a[...], c[...], DN, preferred_element_type=F32) + r[...].astype(F32)
        for o in range(NY):

            @pl.when(pl.program_id(0) == o)
            def _():
                outs[o][...] = acc.astype(BF16)

    return pl.pallas_call(
        kernel,
        grid_spec=pltpu.PrefetchScalarGridSpec(
            num_scalar_prefetch=1,
            grid=(NY,),
            in_specs=[
                pl.BlockSpec((T, D), lambda j, s: (0, 0)),
                pl.BlockSpec((T, TN), lambda j, s: (0, s[0] * (HALF // TN) + base // TN + lax.rem(s[2] + j, NY))),
                pl.BlockSpec((D, TN), lambda j, s: (0, lax.rem(s[2] + j, NY))),
            ],
            out_specs=[pl.BlockSpec((D, TN), lambda j, s: (0, 0))] * NY,
        ),
        out_shape=[jax.ShapeDtypeStruct((D, TN), BF16)] * NY,
        name="product_for_y",
        **params_of(2 * T * D * TN * NY, 2 * (T * D + T * TN * NY + 2 * D * TN * NY)),
    )(idx, acts, cot, got)


def product_for_x(acts, cot, got, idx, base, ncols):
    def kernel(idx_ref, a, c, r, *rest):
        outs, acc = rest[:NX], rest[NX]
        acc[...] = lax.dot_general(a[...], c[...], DN, preferred_element_type=F32) + r[...].astype(F32)
        for o in range(NX):
            target = lax.rem(idx_ref[1] + o, NX)
            for z in range(NZ):
                rows = pl.ds(pl.multiple_of((z * NX + target) * BLK, BLK), BLK)
                outs[o][z] = acc[rows, :].astype(BF16)

    return pl.pallas_call(
        kernel,
        grid_spec=pltpu.PrefetchScalarGridSpec(
            num_scalar_prefetch=1,
            grid=(ncols // TN,),
            in_specs=[
                pl.BlockSpec((T, D), lambda j, s: (0, 0)),
                pl.BlockSpec((T, TN), lambda j, s: (0, s[0] * (HALF // TN) + base // TN + j)),
                pl.BlockSpec((D, TN), lambda j, s: (0, j)),
            ],
            out_specs=[pl.BlockSpec((NZ, BLK, TN), lambda j, s: (0, 0, j))] * NX,
            scratch_shapes=[pltpu.VMEM((D, TN), F32)],
        ),
        out_shape=[jax.ShapeDtypeStruct((NZ, BLK, ncols), BF16)] * NX,
        name="product_for_x",
        **params_of(2 * T * D * ncols, 2 * (T * D + T * ncols + 2 * D * ncols)),
    )(idx, acts, cot, got)


def sum_for_x(parts, idx):
    width = parts[0].shape[-1]

    def kernel(idx_ref, *refs):
        ins, outs = refs[:NY], refs[NY:]
        total = ins[0][...].astype(F32)
        for r in ins[1:]:
            total = total + r[...].astype(F32)
        for o in range(NX):

            @pl.when(pl.program_id(0) == o)
            def _():
                outs[o][...] = total[:, 0].astype(BF16)

    return pl.pallas_call(
        kernel,
        grid_spec=pltpu.PrefetchScalarGridSpec(
            num_scalar_prefetch=1,
            grid=(NX,),
            in_specs=[pl.BlockSpec((NZ, 1, BLK, width), lambda j, s: (0, lax.rem(s[1] + j, NX), 0, 0))] * NY,
            out_specs=[pl.BlockSpec((NZ, BLK, width), lambda j, s: (0, 0, 0))] * NX,
        ),
        out_shape=[jax.ShapeDtypeStruct((NZ, BLK, width), BF16)] * NX,
        name="sum_for_x",
        **params_of(4 * D * width, 2 * 5 * D * width),
    )(idx, *[p.reshape(NZ, NX, BLK, width) for p in parts])


def sum_for_z(first, second, idx):
    wa, wb = first[0].shape[-1], second[0].shape[-1]

    def kernel(idx_ref, *refs):
        ins, outs = refs[: 2 * NX], refs[2 * NX :]
        sums = []
        for group in (ins[:NX], ins[NX:]):
            total = group[0][0].astype(F32)
            for r in group[1:]:
                total = total + r[0].astype(F32)
            sums.append(total.astype(BF16))
        for o in range(NZ):

            @pl.when(pl.program_id(0) == o)
            def _():
                outs[o][:, :wa] = sums[0]
                outs[o][:, wa:] = sums[1]

    spec = lambda w: pl.BlockSpec((1, BLK, w), lambda j, s: (lax.rem(s[3] + j, NZ), 0, 0))
    return pl.pallas_call(
        kernel,
        grid_spec=pltpu.PrefetchScalarGridSpec(
            num_scalar_prefetch=1,
            grid=(NZ,),
            in_specs=[spec(wa)] * NX + [spec(wb)] * NX,
            out_specs=[pl.BlockSpec((BLK, wa + wb), lambda j, s: (0, 0))] * NZ,
        ),
        out_shape=[jax.ShapeDtypeStruct((BLK, wa + wb), BF16)] * NZ,
        name="sum_for_z",
        **params_of(4 * NZ * BLK * (wa + wb), 2 * 5 * NZ * BLK * (wa + wb)),
    )(idx, *first, *second)


def sum_for_core(parts, idx):
    width = parts[0].shape[-1]
    rows = BLK // NC

    def kernel(idx_ref, *refs):
        ins, mine, theirs, acc = refs[:NZ], refs[NZ], refs[NZ + 1], refs[NZ + 2]
        total = ins[0][...].astype(F32)
        for r in ins[1:]:
            total = total + r[...].astype(F32)
        acc[...] = total
        c = idx_ref[0]
        mine[...] = acc[pl.ds(pl.multiple_of(c * rows, rows), rows), :].astype(BF16)
        theirs[...] = acc[pl.ds(pl.multiple_of((1 - c) * rows, rows), rows), :].astype(BF16)

    whole = lambda h: pl.BlockSpec((h, width), lambda j, s: (0, 0))
    return pl.pallas_call(
        kernel,
        grid_spec=pltpu.PrefetchScalarGridSpec(
            num_scalar_prefetch=1,
            grid=(1,),
            in_specs=[whole(BLK)] * NZ,
            out_specs=[whole(rows)] * NC,
            scratch_shapes=[pltpu.VMEM((BLK, width), F32)],
        ),
        out_shape=[jax.ShapeDtypeStruct((rows, width), BF16)] * NC,
        name="sum_for_core",
        **params_of(NZ * BLK * width, 2 * 9 * BLK * width),
    )(idx, *parts)


def body(acts, cotangent, master, moment, second):
    z, x, c, y = (lax.axis_index(a) for a in ("z", "x", "c", "y"))
    idx = jnp.stack([c, x, y, z]).astype(jnp.int32)
    theirs_c = product(acts, cotangent, idx, 0, FLOW_C)
    got_c = shift(theirs_c, "c", NC, 1)
    theirs_b = product(acts, cotangent, idx, FLOW_C, FLOW_B)
    got_b = shift(theirs_b, "c", NC, 1)
    pieces_c = product_for_y(acts, cotangent, got_c, idx, 0)
    over_y = [pieces_c[0]] + [shift(pieces_c[s], "y", NY, s) for s in (1, 3, 2)]
    pieces_b = product_for_x(acts, cotangent, got_b, idx, FLOW_C, FLOW_B)
    over_x = [pieces_b[0]] + [shift(pieces_b[s], "x", NX, s) for s in (1, 3, 2)]
    pieces_cx = sum_for_x(over_y, idx)
    over_cx = [pieces_cx[0]] + [shift(pieces_cx[s], "x", NX, s) for s in (1, 3, 2)]
    pieces_z = sum_for_z(over_cx, over_x, idx)
    over_z = [pieces_z[0]] + [shift(pieces_z[s], "z", NZ, s) for s in (4, 3, 5, 2, 6, 1, 7)]
    mine, theirs = sum_for_core(over_z, idx)
    got = shift(theirs, "c", NC, 1)
    pair = jnp.stack([jnp.where(c == 0, mine, got), jnp.where(c == 0, got, mine)])
    rows = BLK // NC // NY
    piece = lambda s: lax.dynamic_slice_in_dim(pair, lax.rem(y + s, NY) * rows, rows, 1)
    from_y = [piece(0)] + [shift(piece(s), "y", NY, s) for s in (1, 2, 3)]
    width = FLOW_C // NY
    by_source = [lax.select_n(lax.rem(y - k + NY, NY), *[p[:, :, :width] for p in from_y]) for k in range(NY)]
    part_c = jnp.concatenate(by_source, axis=-1).astype(F32)
    part_b = sum(p[:, :, width:].astype(F32) for p in from_y)
    halves = jnp.concatenate([part_c, part_b], axis=-1)
    grad = jnp.concatenate([halves[0], halves[1]], axis=-1)
    new_moment = 0.9 * moment + 0.1 * grad
    new_second = 0.95 * second + 0.05 * grad * grad
    corr_one = 1.0 - 0.9**10
    corr_two = 1.0 - 0.95**10
    update = new_moment / corr_one / (jnp.sqrt(new_second / corr_two) + 1e-08)
    new_master = master - 0.02 * (update + 0.1 * master)
    rounded = new_master.astype(BF16)
    every = [rounded] + [shift(rounded, "y", NY, s) for s in (1, 2, 3)]
    params = jnp.concatenate([lax.select_n(lax.rem(y - k + NY, NY), *every) for k in range(NY)], axis=0)
    return (new_master, new_moment, new_second, params)


def solution(mesh):
    fine = Mesh(mesh.devices.reshape(NZ, NX, NC, NY), ("z", "x", "c", "y"))
    split = P(("z", "x", "c", "y"), None)
    return jax.shard_map(
        body,
        mesh=fine,
        in_specs=(split,) * 5,
        out_specs=(split, split, split, P(("z", "x", "c"), None)),
        check_vma=False,
    )
```

```python
import jax
import jax.numpy as jnp
from jax import lax
from jax.experimental import pallas as pl
from jax.experimental.pallas import tpu as pltpu
from jax.sharding import Mesh, PartitionSpec as P

NZ, NX, NC, NY = 8, 4, 2, 4
D, FFW = 1536, 4096
W = 128
FLOWS = FFW // NC // NY // W
BLK = D // (NZ * NX)
ROWS = BLK // NC
OWN = ROWS // NY
T = 1024
MT = 384
F32, BF16 = jnp.float32, jnp.bfloat16
VMEM_LIMIT = 32 * 1024 * 1024
DN = (((0,), (0,)), ((), ()))


def params_of(flops, nbytes):
    return dict(
        compiler_params=pltpu.CompilerParams(vmem_limit_bytes=VMEM_LIMIT),
        cost_estimate=pl.CostEstimate(flops=flops // 64, bytes_accessed=nbytes // 64, transcendentals=0),
    )


def shift(v, axis, n, s):
    return lax.ppermute(v, axis, [(i, (i + s) % n) for i in range(n)])


def exchange(pieces, axis, n, order):
    return [pieces[0]] + [shift(pieces[s], axis, n, s) for s in order]


def cot_specs(first, count, other):
    per_y, width = FLOWS // count, count * W

    def spec(y):
        def place(j, s):
            core = 1 - s[0] if other else s[0]
            return (0, (core * NY + y) * per_y + first // count)

        return pl.BlockSpec((T, width), place)

    return [spec(y) for y in range(NY)]


def gather_cot(refs, cot):
    @pl.when(pl.program_id(0) == 0)
    def _():
        width = cot.shape[1] // NY
        for y in range(NY):
            cot[:, y * width : (y + 1) * width] = refs[y][...]


def product_theirs(acts, cot, idx, first, count, after=()):
    n = NY * count * W

    def kernel(idx_ref, a, *rest):
        cots, o, scratch = rest[:NY], rest[-2], rest[-1]
        gather_cot(cots, scratch)
        o[...] = lax.dot_general(a[...], scratch[...], DN, preferred_element_type=F32).astype(BF16)

    return pl.pallas_call(
        kernel,
        grid_spec=pltpu.PrefetchScalarGridSpec(
            num_scalar_prefetch=1,
            grid=(D // MT,),
            in_specs=[pl.BlockSpec((T, MT), lambda j, s: (0, j))]
            + cot_specs(first, count, True)
            + [pl.BlockSpec(memory_space=pl.ANY)] * len(after),
            out_specs=pl.BlockSpec((MT, n), lambda j, s: (j, 0)),
            scratch_shapes=[pltpu.VMEM((T, n), BF16)],
        ),
        out_shape=jax.ShapeDtypeStruct((D, n), BF16),
        name="product_theirs",
        **params_of(2 * T * D * n, 2 * (T * D + T * n + D * n)),
    )(idx, acts, *[cot] * NY, *after)


def product_mine(acts, cot, got, idx, first, kinds):
    count = len(kinds)
    n = NY * count * W

    def kernel(idx_ref, a, *rest):
        cots, r, outs, scratch, acc = rest[:NY], rest[NY], rest[NY + 1 : -2], rest[-2], rest[-1]
        gather_cot(cots, scratch)
        acc[...] = lax.dot_general(a[...], scratch[...], DN, preferred_element_type=F32) + r[...].astype(F32)
        outs = list(outs)
        for k, kind in enumerate(kinds):
            for o in range(4):
                out = outs.pop(0)
                if kind == "y":
                    target = lax.rem(idx_ref[2] + o, NY)
                    columns = pl.ds(pl.multiple_of((target * count + k) * W, W), W)
                    out[...] = acc[:, columns].astype(BF16)
                else:
                    target = lax.rem(idx_ref[1] + o, NX)
                    for z in range(MT // (NX * BLK)):
                        rows = pl.ds(pl.multiple_of((z * NX + target) * BLK, BLK), BLK)
                        for y in range(NY):
                            out[z, :, y * W : (y + 1) * W] = acc[
                                rows, (y * count + k) * W : (y * count + k + 1) * W
                            ].astype(BF16)

    out_specs, out_shape = [], []
    for kind in kinds:
        for o in range(4):
            if kind == "y":
                out_specs.append(pl.BlockSpec((MT, W), lambda j, s: (j, 0)))
                out_shape.append(jax.ShapeDtypeStruct((D, W), BF16))
            else:
                out_specs.append(pl.BlockSpec((MT // (NX * BLK), BLK, NY * W), lambda j, s: (j, 0, 0)))
                out_shape.append(jax.ShapeDtypeStruct((NZ, BLK, NY * W), BF16))
    outs = pl.pallas_call(
        kernel,
        grid_spec=pltpu.PrefetchScalarGridSpec(
            num_scalar_prefetch=1,
            grid=(D // MT,),
            in_specs=[pl.BlockSpec((T, MT), lambda j, s: (0, j))]
            + cot_specs(first, count, False)
            + [pl.BlockSpec((MT, n), lambda j, s: (j, 0))],
            out_specs=out_specs,
            scratch_shapes=[pltpu.VMEM((T, n), BF16), pltpu.VMEM((MT, n), F32)],
        ),
        out_shape=out_shape,
        name="product_mine",
        **params_of(2 * T * D * n, 2 * (T * D + T * n + 2 * D * n)),
    )(idx, acts, *[cot] * NY, got)
    return [outs[4 * k : 4 * k + 4] for k in range(count)]


def sum_and_cut(parts, idx, kind, after=()):
    if kind == "x":
        parts = [p.reshape(NZ, NX, BLK, W) for p in parts]
        spec = pl.BlockSpec((NZ, 1, BLK, W), lambda j, s: (0, lax.rem(s[1] + j, NX), 0, 0))
    else:
        spec = pl.BlockSpec((NZ, BLK, W), lambda j, s: (0, 0, lax.rem(s[2] + j, NY)))

    def kernel(idx_ref, *refs):
        ins, outs = refs[:4], refs[4 + len(after) :]
        total = ins[0][...].astype(F32)
        for r in ins[1:]:
            total = total + r[...].astype(F32)
        total = total.reshape(NZ, BLK, W).astype(BF16)
        for o in range(4):

            @pl.when(pl.program_id(0) == o)
            def _():
                outs[o][...] = total

    return pl.pallas_call(
        kernel,
        grid_spec=pltpu.PrefetchScalarGridSpec(
            num_scalar_prefetch=1,
            grid=(4,),
            in_specs=[spec] * 4 + [pl.BlockSpec(memory_space=pl.ANY)] * len(after),
            out_specs=[pl.BlockSpec((NZ, BLK, W), lambda j, s: (0, 0, 0))] * 4,
        ),
        out_shape=[jax.ShapeDtypeStruct((NZ, BLK, W), BF16)] * 4,
        name="sum_and_cut_" + kind,
        **params_of(16 * NZ * BLK * W, 40 * NZ * BLK * W),
    )(idx, *parts, *after)


def sum_for_z(groups, idx):
    width = len(groups) * W

    def kernel(idx_ref, *refs):
        ins, outs = refs[: 4 * len(groups)], refs[4 * len(groups) :]
        sums = []
        for g in range(len(groups)):
            total = ins[4 * g][0].astype(F32)
            for r in ins[4 * g + 1 : 4 * g + 4]:
                total = total + r[0].astype(F32)
            sums.append(total.astype(BF16))
        for o in range(NZ):

            @pl.when(pl.program_id(0) == o)
            def _():
                for g, total in enumerate(sums):
                    outs[o][:, g * W : (g + 1) * W] = total

    spec = pl.BlockSpec((1, BLK, W), lambda j, s: (lax.rem(s[3] + j, NZ), 0, 0))
    return pl.pallas_call(
        kernel,
        grid_spec=pltpu.PrefetchScalarGridSpec(
            num_scalar_prefetch=1,
            grid=(NZ,),
            in_specs=[spec] * (4 * len(groups)),
            out_specs=[pl.BlockSpec((BLK, width), lambda j, s: (0, 0))] * NZ,
        ),
        out_shape=[jax.ShapeDtypeStruct((BLK, width), BF16)] * NZ,
        name="sum_for_z",
        **params_of(4 * NZ * BLK * width, 10 * NZ * BLK * width),
    )(idx, *[p for group in groups for p in group])


def sum_for_core(parts, idx):
    width = parts[0].shape[-1]

    def kernel(idx_ref, *refs):
        ins, mine, theirs, acc = refs[:NZ], refs[NZ], refs[NZ + 1], refs[NZ + 2]
        total = ins[0][...].astype(F32)
        for r in ins[1:]:
            total = total + r[...].astype(F32)
        acc[...] = total
        c = idx_ref[0]
        mine[...] = acc[pl.ds(pl.multiple_of(c * ROWS, ROWS), ROWS), :].astype(BF16)
        theirs[...] = acc[pl.ds(pl.multiple_of((1 - c) * ROWS, ROWS), ROWS), :].astype(BF16)

    whole = lambda h: pl.BlockSpec((h, width), lambda j, s: (0, 0))
    return pl.pallas_call(
        kernel,
        grid_spec=pltpu.PrefetchScalarGridSpec(
            num_scalar_prefetch=1,
            grid=(1,),
            in_specs=[whole(BLK)] * NZ,
            out_specs=[whole(ROWS)] * NC,
            scratch_shapes=[pltpu.VMEM((BLK, width), F32)],
        ),
        out_shape=[jax.ShapeDtypeStruct((ROWS, width), BF16)] * NC,
        name="sum_for_core",
        **params_of(NZ * BLK * width, 2 * 9 * BLK * width),
    )(idx, *parts)


def adamw(grad, master, moment, second):
    new_moment = 0.9 * moment + 0.1 * grad
    new_second = 0.95 * second + 0.05 * grad * grad
    corr_one = 1.0 - 0.9**10
    corr_two = 1.0 - 0.95**10
    update = new_moment / corr_one / (jnp.sqrt(new_second / corr_two) + 1e-08)
    return master - 0.02 * (update + 0.1 * master), new_moment, new_second


def finish(pairs, state, master, moment, second, idx):
    width = FLOWS * W

    def kernel(idx_ref, *refs):
        ins, st, own, outs, grad = refs[:NY], refs[NY], refs[NY + 1 : NY + 4], refs[NY + 4 : NY + 8], refs[NY + 8]
        y = idx_ref[2]
        for s in range(NY):
            source = lax.rem(y - s + NY, NY)
            for h in range(NC):
                columns = pl.ds(pl.multiple_of((h * NY + source) * width, width), width)
                grad[:, columns] = ins[s][h * ROWS : (h + 1) * ROWS, :].astype(F32)
        new_params, _, _ = adamw(grad[...], st[0], st[1], st[2])
        outs[3][...] = new_params.astype(BF16)
        for k in range(NY):

            @pl.when(y == k)
            def _():
                results = adamw(grad[k * OWN : (k + 1) * OWN, :], *[r[...] for r in own])
                for out, value in zip(outs, results):
                    out[...] = value

    whole = lambda *shape: pl.BlockSpec(shape, lambda j, s: (0,) * len(shape))
    return pl.pallas_call(
        kernel,
        grid_spec=pltpu.PrefetchScalarGridSpec(
            num_scalar_prefetch=1,
            grid=(1,),
            in_specs=[whole(NC * ROWS, width)] * NY + [whole(3, ROWS, FFW)] + [whole(OWN, FFW)] * 3,
            out_specs=[whole(OWN, FFW)] * 3 + [whole(ROWS, FFW)],
            scratch_shapes=[pltpu.VMEM((ROWS, FFW), F32)],
        ),
        out_shape=[jax.ShapeDtypeStruct((OWN, FFW), F32)] * 3 + [jax.ShapeDtypeStruct((ROWS, FFW), BF16)],
        name="finish",
        **params_of(20 * ROWS * FFW, 20 * ROWS * FFW),
    )(idx, *pairs, state, master, moment, second)


def body(acts, cotangent, master, moment, second):
    z, x, c, y = (lax.axis_index(a) for a in ("z", "x", "c", "y"))
    idx = jnp.stack([c, x, y, z]).astype(jnp.int32)
    ordered = lambda every: [lax.select_n(lax.rem(y - k + NY, NY), *every) for k in range(NY)]

    high = master.astype(BF16)
    low = (master - high.astype(F32)).astype(BF16)
    state = jnp.stack([high, low, moment.astype(BF16), second.astype(BF16)])
    states = exchange([state] * NY, "y", NY, (1, 2, 3))
    rows = jnp.concatenate(ordered(states), axis=1).astype(F32)
    state = jnp.stack([rows[0] + rows[1], rows[2], rows[3]])

    theirs_0 = product_theirs(acts, cotangent, idx, 0, 1)
    got_0 = shift(theirs_0, "c", NC, 1)
    theirs_1 = product_theirs(acts, cotangent, idx, 1, 1)
    got_1 = shift(theirs_1, "c", NC, 1)
    (cut_0,) = product_mine(acts, cotangent, got_0, idx, 0, "y")
    (cut_1,) = product_mine(acts, cotangent, got_1, idx, 1, "x")
    theirs_2 = product_theirs(acts, cotangent, idx, 2, 2, (cut_0[0], cut_1[0], *states[1:]))
    got_2 = shift(theirs_2, "c", NC, 1)
    cut_2, cut_3 = product_mine(acts, cotangent, got_2, idx, 2, "yx")
    groups = []
    for n, (cut, kind) in enumerate(((cut_0, "y"), (cut_1, "x"), (cut_2, "y"), (cut_3, "x"))):
        other = "x" if kind == "y" else "y"
        arrived = exchange(cut, kind, 4, (1, 3, 2))
        summed = sum_and_cut(arrived, idx, other, (state,) if n == 2 else ())
        groups.append(exchange(summed, other, 4, (1, 3, 2)))
    mine, theirs = sum_for_core(exchange(sum_for_z(groups, idx), "z", NZ, (4, 3, 5, 2, 6, 1, 7)), idx)
    got = shift(theirs, "c", NC, 1)
    pair = jnp.concatenate([jnp.where(c == 0, mine, got), jnp.where(c == 0, got, mine)], axis=0)
    return tuple(finish(exchange([pair] * NY, "y", NY, (1, 2, 3)), state, master, moment, second, idx))


def solution(mesh):
    fine = Mesh(mesh.devices.reshape(NZ, NX, NC, NY), ("z", "x", "c", "y"))
    split = P(("z", "x", "c", "y"), None)
    return jax.shard_map(
        body,
        mesh=fine,
        in_specs=(split,) * 5,
        out_specs=(split, split, split, P(("z", "x", "c"), None)),
        check_vma=False,
    )
```

```python
import jax
import jax.numpy as jnp
from jax import lax
from jax.experimental import pallas as pl
from jax.experimental.pallas import tpu as pltpu
from jax.sharding import Mesh, PartitionSpec as P

NZ, NX, NC, NY = 8, 4, 2, 4
D, FFW = 1536, 4096
W = 128
FLOWS = FFW // NC // NY // W
BLK = D // (NZ * NX)
ROWS = BLK // NC
OWN = ROWS // NY
T = 1024
MT = 384
F32, BF16 = jnp.float32, jnp.bfloat16
VMEM_LIMIT = 62 * 1024 * 1024
DN = (((0,), (0,)), ((), ()))


def params_of(flops, nbytes):
    return dict(
        compiler_params=pltpu.CompilerParams(vmem_limit_bytes=VMEM_LIMIT),
        cost_estimate=pl.CostEstimate(flops=flops // 64, bytes_accessed=nbytes // 64, transcendentals=0),
    )


def shift(v, axis, n, s):
    return lax.ppermute(v, axis, [(i, (i + s) % n) for i in range(n)])


def exchange(pieces, axis, n, order):
    return [pieces[0]] + [shift(pieces[s], axis, n, s) for s in order]


def cot_specs(first, count, other):
    per_y, width = FLOWS // count, count * W

    def spec(y):
        def place(j, s):
            core = 1 - s[0] if other else s[0]
            return (0, (core * NY + y) * per_y + first // count)

        return pl.BlockSpec((T, width), place)

    return [spec(y) for y in range(NY)]


def gather_cot(refs, cot):
    @pl.when(pl.program_id(0) == 0)
    def _():
        width = cot.shape[1] // NY
        for y in range(NY):
            cot[:, y * width : (y + 1) * width] = refs[y][...]


def product_theirs(acts, cot, idx, first, count, after=()):
    n = NY * count * W

    def kernel(idx_ref, a, *rest):
        cots, o, scratch = rest[:NY], rest[-2], rest[-1]
        gather_cot(cots, scratch)
        o[...] = lax.dot_general(a[...], scratch[...], DN, preferred_element_type=F32).astype(BF16)

    return pl.pallas_call(
        kernel,
        grid_spec=pltpu.PrefetchScalarGridSpec(
            num_scalar_prefetch=1,
            grid=(D // MT,),
            in_specs=[pl.BlockSpec((T, MT), lambda j, s: (0, j))]
            + cot_specs(first, count, True)
            + [pl.BlockSpec(memory_space=pl.ANY)] * len(after),
            out_specs=pl.BlockSpec((MT, n), lambda j, s: (j, 0)),
            scratch_shapes=[pltpu.VMEM((T, n), BF16)],
        ),
        out_shape=jax.ShapeDtypeStruct((D, n), BF16),
        name="product_theirs",
        **params_of(2 * T * D * n, 2 * (T * D + T * n + D * n)),
    )(idx, acts, *[cot] * NY, *after)


def product_mine(acts, cot, got, idx, first, kinds):
    count = len(kinds)
    n = NY * count * W

    def kernel(idx_ref, a, *rest):
        cots, r, outs, scratch, acc = rest[:NY], rest[NY], rest[NY + 1 : -2], rest[-2], rest[-1]
        gather_cot(cots, scratch)
        acc[...] = lax.dot_general(a[...], scratch[...], DN, preferred_element_type=F32) + r[...].astype(F32)
        outs = list(outs)
        for k, kind in enumerate(kinds):
            for o in range(4):
                out = outs.pop(0)
                if kind == "y":
                    target = lax.rem(idx_ref[2] + o, NY)
                    columns = pl.ds(pl.multiple_of((target * count + k) * W, W), W)
                    out[...] = acc[:, columns].astype(BF16)
                else:
                    target = lax.rem(idx_ref[1] + o, NX)
                    for z in range(MT // (NX * BLK)):
                        rows = pl.ds(pl.multiple_of((z * NX + target) * BLK, BLK), BLK)
                        for y in range(NY):
                            out[z, :, y * W : (y + 1) * W] = acc[
                                rows, (y * count + k) * W : (y * count + k + 1) * W
                            ].astype(BF16)

    out_specs, out_shape = [], []
    for kind in kinds:
        for o in range(4):
            if kind == "y":
                out_specs.append(pl.BlockSpec((MT, W), lambda j, s: (j, 0)))
                out_shape.append(jax.ShapeDtypeStruct((D, W), BF16))
            else:
                out_specs.append(pl.BlockSpec((MT // (NX * BLK), BLK, NY * W), lambda j, s: (j, 0, 0)))
                out_shape.append(jax.ShapeDtypeStruct((NZ, BLK, NY * W), BF16))
    outs = pl.pallas_call(
        kernel,
        grid_spec=pltpu.PrefetchScalarGridSpec(
            num_scalar_prefetch=1,
            grid=(D // MT,),
            in_specs=[pl.BlockSpec((T, MT), lambda j, s: (0, j))]
            + cot_specs(first, count, False)
            + [pl.BlockSpec((MT, n), lambda j, s: (j, 0))],
            out_specs=out_specs,
            scratch_shapes=[pltpu.VMEM((T, n), BF16), pltpu.VMEM((MT, n), F32)],
        ),
        out_shape=out_shape,
        name="product_mine",
        **params_of(2 * T * D * n, 2 * (T * D + T * n + 2 * D * n)),
    )(idx, acts, *[cot] * NY, got)
    return [outs[4 * k : 4 * k + 4] for k in range(count)]


def sum_and_cut(flows, idx):
    ins, in_specs, starts = [], [], []
    for kind, chunks in flows:
        if kind == "x":
            chunks = [[p.reshape(NZ, NX, BLK, W) for p in parts] for parts in chunks]
            spec = pl.BlockSpec((NZ, 1, BLK, W), lambda j, s: (0, lax.rem(s[1] + j, NX), 0, 0))
        else:
            spec = pl.BlockSpec((NZ, BLK, W), lambda j, s: (0, 0, lax.rem(s[2] + j, NY)))
        starts.append([len(ins) + 4 * n for n in range(len(chunks))])
        for parts in chunks:
            ins += parts
            in_specs += [spec] * 4
    width = len(flows[0][1]) * W

    def kernel(idx_ref, *refs):
        outs = refs[len(ins) :]
        for f, places in enumerate(starts):
            sums = []
            for n in places:
                total = refs[n][...].astype(F32)
                for r in refs[n + 1 : n + 4]:
                    total = total + r[...].astype(F32)
                sums.append(total.reshape(NZ, BLK, W).astype(BF16))
            for o in range(4):

                @pl.when(pl.program_id(0) == o)
                def _():
                    for n, total in enumerate(sums):
                        outs[4 * f + o][:, :, n * W : (n + 1) * W] = total

    outs = pl.pallas_call(
        kernel,
        grid_spec=pltpu.PrefetchScalarGridSpec(
            num_scalar_prefetch=1,
            grid=(4,),
            in_specs=in_specs,
            out_specs=[pl.BlockSpec((NZ, BLK, width), lambda j, s: (0, 0, 0))] * (4 * len(flows)),
        ),
        out_shape=[jax.ShapeDtypeStruct((NZ, BLK, width), BF16)] * (4 * len(flows)),
        name="sum_and_cut",
        **params_of(16 * NZ * BLK * width * len(flows), 40 * NZ * BLK * width * len(flows)),
    )(idx, *ins)
    return [outs[4 * f : 4 * f + 4] for f in range(len(flows))]


def sum_for_z(groups):
    count = len(groups)
    chunks = groups[0][0].shape[-1] // W

    def kernel(*refs):
        ins, out = refs[:-1], refs[-1]
        for g in range(count):
            total = ins[4 * g][0].astype(F32)
            for r in ins[4 * g + 1 : 4 * g + 4]:
                total = total + r[0].astype(F32)
            for n in range(chunks):
                f = n * count + g
                out[0, :, f * W : (f + 1) * W] = total[:, n * W : (n + 1) * W].astype(BF16)

    width = FLOWS * W
    return pl.pallas_call(
        kernel,
        grid=(NZ,),
        in_specs=[pl.BlockSpec((1, BLK, chunks * W), lambda j: (j, 0, 0))] * (4 * count),
        out_specs=pl.BlockSpec((1, BLK, width), lambda j: (j, 0, 0)),
        out_shape=jax.ShapeDtypeStruct((NZ, BLK, width), BF16),
        name="sum_for_z",
        **params_of(4 * NZ * BLK * width, 10 * NZ * BLK * width),
    )(*[p for group in groups for p in group])


def adamw(grad, master, moment, second):
    new_moment = 0.9 * moment + 0.1 * grad
    new_second = 0.95 * second + 0.05 * grad * grad
    corr_one = 1.0 - 0.9**10
    corr_two = 1.0 - 0.95**10
    update = new_moment / corr_one / (jnp.sqrt(new_second / corr_two) + 1e-08)
    return master - 0.02 * (update + 0.1 * master), new_moment, new_second


def body(acts, cotangent, master, moment, second):
    z, x, c, y = (lax.axis_index(a) for a in ("z", "x", "c", "y"))
    idx = jnp.stack([c, x, y, z]).astype(jnp.int32)

    theirs = [product_theirs(acts, cotangent, idx, first, 2) for first in (0, 2)]
    got = [shift(p, "c", NC, 1) for p in theirs]
    cuts = [product_mine(acts, cotangent, g, idx, first, "yx") for g, first in zip(got, (0, 2))]
    near = [[exchange(cut, kind, 4, (1, 3, 2)) for cut, kind in zip(pair, "yx")] for pair in cuts]
    for_x, for_y = sum_and_cut((("x", [p[0] for p in near]), ("y", [p[1] for p in near])), idx)
    over_x = exchange(for_x, "x", 4, (1, 3, 2))
    over_y = exchange(for_y, "y", 4, (1, 3, 2))
    over_z = lax.all_to_all(sum_for_z([over_x, over_y]), "z", 0, 0, tiled=True)
    rows = jnp.sum(over_z.astype(F32), axis=0).astype(BF16).reshape(NC * NY, OWN, FLOWS * W)
    pieces = lax.all_to_all(rows, ("c", "y"), 0, 0, tiled=True)
    grad = jnp.concatenate([pieces[k] for k in range(NC * NY)], axis=-1).astype(F32)

    new_master, new_moment, new_second = adamw(grad, master, moment, second)
    every = exchange([new_master.astype(BF16)] * NY, "y", NY, (1, 2, 3))
    params = jnp.concatenate([lax.select_n(lax.rem(y - k + NY, NY), *every) for k in range(NY)], axis=0)
    return (new_master, new_moment, new_second, params)


def solution(mesh):
    fine = Mesh(mesh.devices.reshape(NZ, NX, NC, NY), ("z", "x", "c", "y"))
    split = P(("z", "x", "c", "y"), None)
    return jax.shard_map(
        body,
        mesh=fine,
        in_specs=(split,) * 5,
        out_specs=(split, split, split, P(("z", "x", "c"), None)),
        check_vma=False,
    )
```

```python
import jax
import jax.numpy as jnp
from jax import lax
from jax.experimental import pallas as pl
from jax.experimental.pallas import tpu as pltpu
from jax.sharding import Mesh, PartitionSpec as P

NZ, NX, NC, NY = 8, 4, 2, 4
D, FFW = 1536, 4096
HALF = FFW // 2
TN = 256
BLK = D // (NZ * NX)
FLOW_C = 1024
FLOW_A = 1024
T = 1024
F32, BF16 = jnp.float32, jnp.bfloat16
VMEM_LIMIT = 62 * 1024 * 1024
DN = (((0,), (0,)), ((), ()))


def params_of(flops, nbytes):
    return dict(
        compiler_params=pltpu.CompilerParams(vmem_limit_bytes=VMEM_LIMIT),
        cost_estimate=pl.CostEstimate(flops=flops, bytes_accessed=nbytes, transcendentals=0),
    )


def shift(v, axis, n, s):
    return lax.ppermute(v, axis, [(i, (i + s) % n) for i in range(n)])


def product(acts, cot, idx, base, ncols):
    tn = 2 * TN

    def kernel(idx_ref, a, c, o):
        o[...] = lax.dot_general(a[...], c[...], DN, preferred_element_type=F32).astype(BF16)

    return pl.pallas_call(
        kernel,
        grid_spec=pltpu.PrefetchScalarGridSpec(
            num_scalar_prefetch=1,
            grid=(ncols // tn,),
            in_specs=[
                pl.BlockSpec((T, D), lambda j, s: (0, 0)),
                pl.BlockSpec((T, tn), lambda j, s: (0, (1 - s[0]) * (HALF // tn) + base // tn + j)),
            ],
            out_specs=pl.BlockSpec((D, tn), lambda j, s: (0, j)),
        ),
        out_shape=jax.ShapeDtypeStruct((D, ncols), BF16),
        name="product_theirs",
        **params_of(2 * T * D * ncols, 2 * (T * D + T * ncols + D * ncols)),
    )(idx, acts, cot)


def product_for_z(acts, cot, got, idx, base, ncols):
    tn = 2 * TN

    def kernel(idx_ref, a, c, r, o):
        acc = lax.dot_general(a[...], c[...], DN, preferred_element_type=F32) + r[...].astype(F32)
        o[...] = acc.astype(BF16)

    return pl.pallas_call(
        kernel,
        grid_spec=pltpu.PrefetchScalarGridSpec(
            num_scalar_prefetch=1,
            grid=(ncols // tn,),
            in_specs=[
                pl.BlockSpec((T, D), lambda j, s: (0, 0)),
                pl.BlockSpec((T, tn), lambda j, s: (0, s[0] * (HALF // tn) + base // tn + j)),
                pl.BlockSpec((D, tn), lambda j, s: (0, j)),
            ],
            out_specs=pl.BlockSpec((D, tn), lambda j, s: (0, j)),
        ),
        out_shape=jax.ShapeDtypeStruct((D, ncols), BF16),
        name="product_for_z",
        **params_of(2 * T * D * ncols, 2 * (T * D + T * ncols + 2 * D * ncols)),
    )(idx, acts, cot, got)


def product_for_y(acts, cot, got, idx, base):
    def kernel(idx_ref, a, c, r, *outs):
        acc = lax.dot_general(a[...], c[...], DN, preferred_element_type=F32) + r[...].astype(F32)
        for o in range(NY):

            @pl.when(pl.program_id(0) == o)
            def _():
                outs[o][...] = acc.astype(BF16)

    return pl.pallas_call(
        kernel,
        grid_spec=pltpu.PrefetchScalarGridSpec(
            num_scalar_prefetch=1,
            grid=(NY,),
            in_specs=[
                pl.BlockSpec((T, D), lambda j, s: (0, 0)),
                pl.BlockSpec((T, TN), lambda j, s: (0, s[0] * (HALF // TN) + base // TN + lax.rem(s[2] + j, NY))),
                pl.BlockSpec((D, TN), lambda j, s: (0, lax.rem(s[2] + j, NY))),
            ],
            out_specs=[pl.BlockSpec((D, TN), lambda j, s: (0, 0))] * NY,
        ),
        out_shape=[jax.ShapeDtypeStruct((D, TN), BF16)] * NY,
        name="product_for_y",
        **params_of(2 * T * D * TN * NY, 2 * (T * D + T * TN * NY + 2 * D * TN * NY)),
    )(idx, acts, cot, got)


def sum_for_x(parts, idx):
    width = parts[0].shape[-1]

    def kernel(idx_ref, *refs):
        ins, outs = refs[:NY], refs[NY:]
        total = ins[0][...].astype(F32)
        for r in ins[1:]:
            total = total + r[...].astype(F32)
        for o in range(NX):

            @pl.when(pl.program_id(0) == o)
            def _():
                outs[o][...] = total[:, 0].astype(BF16)

    return pl.pallas_call(
        kernel,
        grid_spec=pltpu.PrefetchScalarGridSpec(
            num_scalar_prefetch=1,
            grid=(NX,),
            in_specs=[pl.BlockSpec((NZ, 1, BLK, width), lambda j, s: (0, lax.rem(s[1] + j, NX), 0, 0))] * NY,
            out_specs=[pl.BlockSpec((NZ, BLK, width), lambda j, s: (0, 0, 0))] * NX,
        ),
        out_shape=[jax.ShapeDtypeStruct((NZ, BLK, width), BF16)] * NX,
        name="sum_for_x",
        **params_of(4 * D * width, 2 * 5 * D * width),
    )(idx, *[p.reshape(NZ, NX, BLK, width) for p in parts])


def sum_for_z(parts, idx):
    width = parts[0].shape[-1]

    def kernel(idx_ref, *refs):
        ins, outs = refs[:NX], refs[NX:]
        for o in range(NZ):
            z = lax.rem(idx_ref[3] + o, NZ)
            total = ins[0][z].astype(F32)
            for r in ins[1:]:
                total = total + r[z].astype(F32)
            outs[o][...] = total.astype(BF16)

    return pl.pallas_call(
        kernel,
        grid_spec=pltpu.PrefetchScalarGridSpec(
            num_scalar_prefetch=1,
            grid=(1,),
            in_specs=[pl.BlockSpec((NZ, BLK, width), lambda j, s: (0, 0, 0))] * NX,
            out_specs=[pl.BlockSpec((BLK, width), lambda j, s: (0, 0))] * NZ,
        ),
        out_shape=[jax.ShapeDtypeStruct((BLK, width), BF16)] * NZ,
        name="sum_for_z",
        **params_of(4 * NZ * BLK * width, 10 * NZ * BLK * width),
    )(idx, *parts)


def sum_for_core(first, second, idx):
    wa, wb = first[0].shape[-1], second[0].shape[-1]
    width = wa + wb
    count = len(first) + len(second)
    rows = BLK // NC

    def kernel(idx_ref, *refs):
        mine, theirs, acc = refs[count:]
        for group, columns in ((refs[: len(first)], slice(0, wa)), (refs[len(first) : count], slice(wa, width))):
            total = group[0][...].astype(F32)
            for r in group[1:]:
                total = total + r[...].astype(F32)
            acc[:, columns] = total
        c = idx_ref[0]
        mine[...] = acc[pl.ds(pl.multiple_of(c * rows, rows), rows), :].astype(BF16)
        theirs[...] = acc[pl.ds(pl.multiple_of((1 - c) * rows, rows), rows), :].astype(BF16)

    whole = lambda h, w: pl.BlockSpec((h, w), lambda j, s: (0, 0))
    return pl.pallas_call(
        kernel,
        grid_spec=pltpu.PrefetchScalarGridSpec(
            num_scalar_prefetch=1,
            grid=(1,),
            in_specs=[whole(BLK, wa)] * len(first) + [whole(BLK, wb)] * len(second),
            out_specs=[whole(rows, width)] * NC,
            scratch_shapes=[pltpu.VMEM((BLK, width), F32)],
        ),
        out_shape=[jax.ShapeDtypeStruct((rows, width), BF16)] * NC,
        name="sum_for_core",
        **params_of(NZ * BLK * width, 2 * 9 * BLK * width),
    )(idx, *first, *second)


def body(acts, cotangent, master, moment, second):
    z, x, c, y = (lax.axis_index(a) for a in ("z", "x", "c", "y"))
    idx = jnp.stack([c, x, y, z]).astype(jnp.int32)
    theirs_a = product(acts, cotangent, idx, FLOW_C, FLOW_A)
    got_a = shift(theirs_a, "c", NC, 1)
    theirs_c = product(acts, cotangent, idx, 0, FLOW_C)
    got_c = shift(theirs_c, "c", NC, 1)
    part_a = product_for_z(acts, cotangent, got_a, idx, FLOW_C, FLOW_A)
    part_a = lax.psum_scatter(part_a, "z", scatter_dimension=0, tiled=True).reshape(NX, BLK, FLOW_A)
    pieces_c = product_for_y(acts, cotangent, got_c, idx, 0)
    over_y = [pieces_c[0]] + [shift(pieces_c[s], "y", NY, s) for s in (1, 3, 2)]
    pieces_cx = sum_for_x(over_y, idx)
    over_cx = [pieces_cx[0]] + [shift(pieces_cx[s], "x", NX, s) for s in (1, 3, 2)]
    pieces_z = sum_for_z(over_cx, idx)
    over_z = [pieces_z[0]] + [shift(pieces_z[s], "z", NZ, s) for s in (4, 3, 5, 2, 6, 1, 7)]
    piece_a = lambda s: lax.dynamic_index_in_dim(part_a, lax.rem(x + s, NX), 0, keepdims=False)
    over_ax = [piece_a(0)] + [shift(piece_a(s), "x", NX, s) for s in (1, 3, 2)]
    mine, theirs = sum_for_core(over_z, over_ax, idx)
    got = shift(theirs, "c", NC, 1)
    pair = jnp.stack([jnp.where(c == 0, mine, got), jnp.where(c == 0, got, mine)])
    rows = BLK // NC // NY
    piece = lambda s: lax.dynamic_slice_in_dim(pair, lax.rem(y + s, NY) * rows, rows, 1)
    from_y = [piece(0)] + [shift(piece(s), "y", NY, s) for s in (1, 2, 3)]
    width = FLOW_C // NY
    by_source = [lax.select_n(lax.rem(y - k + NY, NY), *[p[:, :, :width] for p in from_y]) for k in range(NY)]
    part_c = jnp.concatenate(by_source, axis=-1).astype(F32)
    part_b = sum(p[:, :, width:].astype(F32) for p in from_y)
    halves = jnp.concatenate([part_c, part_b], axis=-1)
    grad = jnp.concatenate([halves[0], halves[1]], axis=-1)
    new_moment = 0.9 * moment + 0.1 * grad
    new_second = 0.95 * second + 0.05 * grad * grad
    corr_one = 1.0 - 0.9**10
    corr_two = 1.0 - 0.95**10
    update = new_moment / corr_one / (jnp.sqrt(new_second / corr_two) + 1e-08)
    new_master = master - 0.02 * (update + 0.1 * master)
    rounded = new_master.astype(BF16)
    every = [rounded] + [shift(rounded, "y", NY, s) for s in (1, 2, 3)]
    params = jnp.concatenate([lax.select_n(lax.rem(y - k + NY, NY), *every) for k in range(NY)], axis=0)
    return (new_master, new_moment, new_second, params)


def solution(mesh):
    fine = Mesh(mesh.devices.reshape(NZ, NX, NC, NY), ("z", "x", "c", "y"))
    split = P(("z", "x", "c", "y"), None)
    return jax.shard_map(
        body,
        mesh=fine,
        in_specs=(split,) * 5,
        out_specs=(split, split, split, P(("z", "x", "c"), None)),
        check_vma=False,
    )
```

```python
import jax
import jax.numpy as jnp
from jax import lax
from jax.experimental import pallas as pl
from jax.experimental.pallas import tpu as pltpu
from jax.sharding import Mesh, PartitionSpec as P

NZ, NX, NC, NY = 8, 4, 2, 4
D, FFW = 1536, 4096
HALF = FFW // 2
TN = 256
BLK = D // (NZ * NX)
FLOW_C = 1024
FLOW_A = 1024
T = 1024
F32, BF16 = jnp.float32, jnp.bfloat16
VMEM_LIMIT = 40 * 1024 * 1024
DN = (((0,), (0,)), ((), ()))


def params_of(flops, nbytes):
    return dict(
        compiler_params=pltpu.CompilerParams(vmem_limit_bytes=VMEM_LIMIT),
        cost_estimate=pl.CostEstimate(flops=flops, bytes_accessed=nbytes, transcendentals=0),
    )


def shift(v, axis, n, s):
    return lax.ppermute(v, axis, [(i, (i + s) % n) for i in range(n)])


def swap(v, axes):
    return lax.all_to_all(v, axes, 0, 0, tiled=True)


def product(acts, cot, idx, base, ncols):
    tn = 2 * TN

    def kernel(idx_ref, a, c, o):
        o[...] = lax.dot_general(a[...], c[...], DN, preferred_element_type=F32).astype(BF16)

    return pl.pallas_call(
        kernel,
        grid_spec=pltpu.PrefetchScalarGridSpec(
            num_scalar_prefetch=1,
            grid=(ncols // tn,),
            in_specs=[
                pl.BlockSpec((T, D), lambda j, s: (0, 0)),
                pl.BlockSpec((T, tn), lambda j, s: (0, (1 - s[0]) * (HALF // tn) + base // tn + j)),
            ],
            out_specs=pl.BlockSpec((D, tn), lambda j, s: (0, j)),
        ),
        out_shape=jax.ShapeDtypeStruct((D, ncols), BF16),
        name="product_theirs",
        **params_of(2 * T * D * ncols, 2 * (T * D + T * ncols + D * ncols)),
    )(idx, acts, cot)


def product_for_z(acts, cot, got, idx, base, ncols, after):
    tn = 2 * TN

    def kernel(idx_ref, a, c, r, _, o):
        acc = lax.dot_general(a[...], c[...], DN, preferred_element_type=F32) + r[...].astype(F32)
        o[...] = acc.astype(BF16)

    return pl.pallas_call(
        kernel,
        grid_spec=pltpu.PrefetchScalarGridSpec(
            num_scalar_prefetch=1,
            grid=(ncols // tn,),
            in_specs=[
                pl.BlockSpec((T, D), lambda j, s: (0, 0)),
                pl.BlockSpec((T, tn), lambda j, s: (0, s[0] * (HALF // tn) + base // tn + j)),
                pl.BlockSpec((D, tn), lambda j, s: (0, j)),
                pl.BlockSpec(memory_space=pl.ANY),
            ],
            out_specs=pl.BlockSpec((D, tn), lambda j, s: (0, j)),
        ),
        out_shape=jax.ShapeDtypeStruct((D, ncols), BF16),
        name="product_for_z",
        **params_of(2 * T * D * ncols, 2 * (T * D + T * ncols + 2 * D * ncols)),
    )(idx, acts, cot, got, after)


def product_for_y(acts, cot, got, idx, base):
    def kernel(idx_ref, a, c, r, o):
        acc = lax.dot_general(a[...], c[...], DN, preferred_element_type=F32) + r[...].astype(F32)
        o[0] = acc.astype(BF16)

    return pl.pallas_call(
        kernel,
        grid_spec=pltpu.PrefetchScalarGridSpec(
            num_scalar_prefetch=1,
            grid=(NY,),
            in_specs=[
                pl.BlockSpec((T, D), lambda j, s: (0, 0)),
                pl.BlockSpec((T, TN), lambda j, s: (0, s[0] * (HALF // TN) + base // TN + j)),
                pl.BlockSpec((D, TN), lambda j, s: (0, j)),
            ],
            out_specs=pl.BlockSpec((1, D, TN), lambda j, s: (j, 0, 0)),
        ),
        out_shape=jax.ShapeDtypeStruct((NY, D, TN), BF16),
        name="product_for_y",
        **params_of(2 * T * D * TN * NY, 2 * (T * D + T * TN * NY + 2 * D * TN * NY)),
    )(idx, acts, cot, got)


def sum_for_x(over_y, part_a):
    upper, parts = NZ * BLK, FLOW_A // TN
    height = upper + parts * BLK

    def kernel(c, a, o):
        total = c[0].astype(F32)
        for k in range(1, NY):
            total = total + c[k].astype(F32)
        o[0, :upper, :] = total.reshape(upper, TN).astype(BF16)
        for q in range(parts):
            o[0, upper + q * BLK : upper + (q + 1) * BLK, :] = a[0, :, q * TN : (q + 1) * TN]

    return pl.pallas_call(
        kernel,
        grid=(NX,),
        in_specs=[
            pl.BlockSpec((NY, NZ, 1, BLK, TN), lambda j: (0, 0, j, 0, 0)),
            pl.BlockSpec((1, BLK, FLOW_A), lambda j: (j, 0, 0)),
        ],
        out_specs=pl.BlockSpec((1, height, TN), lambda j: (j, 0, 0)),
        out_shape=jax.ShapeDtypeStruct((NX, height, TN), BF16),
        name="sum_for_x",
        **params_of(4 * D * TN, 10 * D * TN),
    )(over_y.reshape(NY, NZ, NX, BLK, TN), part_a.reshape(NX, BLK, FLOW_A))


def sum_for_z(over_x):
    upper, parts = NZ * BLK, FLOW_A // TN

    def kernel(r, c, a):
        for z in range(NZ + parts):
            rows = slice(z * BLK, (z + 1) * BLK)
            total = r[0, rows, :].astype(F32)
            for k in range(1, NX):
                total = total + r[k, rows, :].astype(F32)
            if z < NZ:
                c[z] = total.astype(BF16)
            else:
                a[:, (z - NZ) * TN : (z - NZ + 1) * TN] = total.astype(BF16)

    whole = lambda *shape: pl.BlockSpec(shape, lambda j: (0,) * len(shape))
    return pl.pallas_call(
        kernel,
        grid=(1,),
        in_specs=[whole(*over_x.shape)],
        out_specs=[whole(NZ, BLK, TN), whole(BLK, FLOW_A)],
        out_shape=[jax.ShapeDtypeStruct((NZ, BLK, TN), BF16), jax.ShapeDtypeStruct((BLK, FLOW_A), BF16)],
        name="sum_for_z",
        **params_of(5 * D * TN, 10 * D * TN),
    )(over_x)


def body(acts, cotangent, master, moment, second):
    y, c = lax.axis_index("y"), lax.axis_index("c")
    idx = jnp.stack([c, y]).astype(jnp.int32)
    theirs_a = product(acts, cotangent, idx, FLOW_C, FLOW_A)
    got_a = shift(theirs_a, "c", NC, 1)
    theirs_c = product(acts, cotangent, idx, 0, FLOW_C)
    got_c = shift(theirs_c, "c", NC, 1)
    part_a = product_for_z(acts, cotangent, got_a, idx, FLOW_C, FLOW_A, theirs_c)
    part_a = lax.psum_scatter(part_a, "z", scatter_dimension=0, tiled=True)
    over_y = swap(product_for_y(acts, cotangent, got_c, idx, 0), "y")
    part_c, part_a = sum_for_z(swap(sum_for_x(over_y, part_a), "x"))
    part_c = jnp.sum(swap(part_c, "z").astype(F32), axis=0).astype(BF16)
    rows = jnp.concatenate([part_c, part_a], axis=-1).reshape(NC * NY, BLK // NC // NY, TN + FLOW_A)
    pieces = swap(rows, ("c", "y"))
    columns = []
    for h in range(NC):
        of_core = [pieces[h * NY + k] for k in range(NY)]
        columns += [p[:, :TN].astype(F32) for p in of_core]
        columns.append(sum(p[:, TN:].astype(F32) for p in of_core))
    grad = jnp.concatenate(columns, axis=-1)
    new_moment = 0.9 * moment + 0.1 * grad
    new_second = 0.95 * second + 0.05 * grad * grad
    corr_one = 1.0 - 0.9**10
    corr_two = 1.0 - 0.95**10
    update = new_moment / corr_one / (jnp.sqrt(new_second / corr_two) + 1e-08)
    new_master = master - 0.02 * (update + 0.1 * master)
    rounded = new_master.astype(BF16)
    every = [rounded] + [shift(rounded, "y", NY, s) for s in (1, 2, 3)]
    params = jnp.concatenate([lax.select_n(lax.rem(y - k + NY, NY), *every) for k in range(NY)], axis=0)
    return (new_master, new_moment, new_second, params)


def solution(mesh):
    fine = Mesh(mesh.devices.reshape(NZ, NX, NC, NY), ("z", "x", "c", "y"))
    split = P(("z", "x", "c", "y"), None)
    return jax.shard_map(
        body,
        mesh=fine,
        in_specs=(split,) * 5,
        out_specs=(split, split, split, P(("z", "x", "c"), None)),
        check_vma=False,
    )
```

```python
import jax
import jax.numpy as jnp
from jax import lax
from jax.experimental import pallas as pl
from jax.experimental.pallas import tpu as pltpu
from jax.sharding import Mesh, PartitionSpec as P

NZ, NX, NC, NY = 8, 4, 2, 4
D, FFW = 1536, 4096
HALF = FFW // 2
TN = 256
BLK = D // (NZ * NX)
FLOW_C = 1024
FLOW_B = 1024
T = 1024
F32, BF16 = jnp.float32, jnp.bfloat16
VMEM_LIMIT = 40 * 1024 * 1024
DN = (((0,), (0,)), ((), ()))


def params_of(flops, nbytes):
    return dict(
        compiler_params=pltpu.CompilerParams(vmem_limit_bytes=VMEM_LIMIT),
        cost_estimate=pl.CostEstimate(flops=flops, bytes_accessed=nbytes, transcendentals=0),
    )


def shift(v, axis, n, s):
    return lax.ppermute(v, axis, [(i, (i + s) % n) for i in range(n)])


def exchange(pieces, axis, n, order):
    return [pieces[0]] + [shift(pieces[s], axis, n, s) for s in order]


def swap(v, axes):
    return lax.all_to_all(v, axes, 0, 0, tiled=True)


def product(acts, cot, idx, base, ncols):
    tn = 2 * TN

    def kernel(idx_ref, a, c, o):
        o[...] = lax.dot_general(a[...], c[...], DN, preferred_element_type=F32).astype(BF16)

    return pl.pallas_call(
        kernel,
        grid_spec=pltpu.PrefetchScalarGridSpec(
            num_scalar_prefetch=1,
            grid=(ncols // tn,),
            in_specs=[
                pl.BlockSpec((T, D), lambda j, s: (0, 0)),
                pl.BlockSpec((T, tn), lambda j, s: (0, (1 - s[0]) * (HALF // tn) + base // tn + j)),
            ],
            out_specs=pl.BlockSpec((D, tn), lambda j, s: (0, j)),
        ),
        out_shape=jax.ShapeDtypeStruct((D, ncols), BF16),
        name="product_theirs",
        **params_of(2 * T * D * ncols, 2 * (T * D + T * ncols + D * ncols)),
    )(idx, acts, cot)


def product_for_y(acts, cot, got, idx, base):
    def kernel(idx_ref, a, c, r, *outs):
        acc = lax.dot_general(a[...], c[...], DN, preferred_element_type=F32) + r[...].astype(F32)
        for o in range(NY):

            @pl.when(pl.program_id(0) == o)
            def _():
                outs[o][...] = acc.astype(BF16)

    return pl.pallas_call(
        kernel,
        grid_spec=pltpu.PrefetchScalarGridSpec(
            num_scalar_prefetch=1,
            grid=(NY,),
            in_specs=[
                pl.BlockSpec((T, D), lambda j, s: (0, 0)),
                pl.BlockSpec((T, TN), lambda j, s: (0, s[0] * (HALF // TN) + base // TN + lax.rem(s[2] + j, NY))),
                pl.BlockSpec((D, TN), lambda j, s: (0, lax.rem(s[2] + j, NY))),
            ],
            out_specs=[pl.BlockSpec((D, TN), lambda j, s: (0, 0))] * NY,
        ),
        out_shape=[jax.ShapeDtypeStruct((D, TN), BF16)] * NY,
        name="product_for_y",
        **params_of(2 * T * D * TN * NY, 2 * (T * D + T * TN * NY + 2 * D * TN * NY)),
    )(idx, acts, cot, got)


def product_for_x(acts, cot, got, idx, base, ncols):
    def kernel(idx_ref, a, c, r, o):
        acc = lax.dot_general(a[...], c[...], DN, preferred_element_type=F32) + r[...].astype(F32)
        acc = acc.astype(BF16).reshape(NZ, NX, BLK, TN)
        for x in range(NX):
            o[x] = acc[:, x]

    return pl.pallas_call(
        kernel,
        grid_spec=pltpu.PrefetchScalarGridSpec(
            num_scalar_prefetch=1,
            grid=(ncols // TN,),
            in_specs=[
                pl.BlockSpec((T, D), lambda j, s: (0, 0)),
                pl.BlockSpec((T, TN), lambda j, s: (0, s[0] * (HALF // TN) + base // TN + j)),
                pl.BlockSpec((D, TN), lambda j, s: (0, j)),
            ],
            out_specs=pl.BlockSpec((NX, NZ, BLK, TN), lambda j, s: (0, 0, 0, j)),
        ),
        out_shape=jax.ShapeDtypeStruct((NX, NZ, BLK, ncols), BF16),
        name="product_for_x",
        **params_of(2 * T * D * ncols, 2 * (T * D + T * ncols + 2 * D * ncols)),
    )(idx, acts, cot, got)


def sum_for_x(parts, idx):
    width = parts[0].shape[-1]

    def kernel(idx_ref, *refs):
        ins, outs = refs[:NY], refs[NY:]
        for o in range(NX):
            x = lax.rem(idx_ref[1] + o, NX)
            for z in range(NZ):
                total = ins[0][z, x].astype(F32)
                for r in ins[1:]:
                    total = total + r[z, x].astype(F32)
                outs[o][z] = total.astype(BF16)

    return pl.pallas_call(
        kernel,
        grid_spec=pltpu.PrefetchScalarGridSpec(
            num_scalar_prefetch=1,
            grid=(1,),
            in_specs=[pl.BlockSpec((NZ, NX, BLK, width), lambda j, s: (0, 0, 0, 0))] * NY,
            out_specs=[pl.BlockSpec((NZ, BLK, width), lambda j, s: (0, 0, 0))] * NX,
        ),
        out_shape=[jax.ShapeDtypeStruct((NZ, BLK, width), BF16)] * NX,
        name="sum_for_x",
        **params_of(4 * D * width, 2 * 5 * D * width),
    )(idx, *[p.reshape(NZ, NX, BLK, width) for p in parts])


def sum_for_y(over_x):
    width = over_x.shape[-1] // NY

    def kernel(r, o):
        total = r[0].astype(F32)
        for k in range(1, NX):
            total = total + r[k].astype(F32)
        o[0] = total.astype(BF16)

    return pl.pallas_call(
        kernel,
        grid=(NY,),
        in_specs=[pl.BlockSpec((NX, NZ, BLK, width), lambda j: (0, 0, 0, j))],
        out_specs=pl.BlockSpec((1, NZ, BLK, width), lambda j: (j, 0, 0, 0)),
        out_shape=jax.ShapeDtypeStruct((NY, NZ, BLK, width), BF16),
        name="sum_for_y",
        **params_of(4 * D * width, 2 * 5 * D * width),
    )(over_x)


def sum_for_z(over_x, over_y):
    width = over_y.shape[-1]

    def kernel(*refs):
        ins, r, o = refs[:NX], refs[NX], refs[NX + 1]
        total = ins[0][...].astype(F32)
        for p in ins[1:]:
            total = total + p[...].astype(F32)
        o[:, :, :width] = total.astype(BF16)
        total = r[0].astype(F32)
        for k in range(1, NY):
            total = total + r[k].astype(F32)
        o[:, :, width:] = total.astype(BF16)

    spec = pl.BlockSpec((NZ // 2, BLK, width), lambda j: (j, 0, 0))
    return pl.pallas_call(
        kernel,
        grid=(2,),
        in_specs=[spec] * NX + [pl.BlockSpec((NY, NZ // 2, BLK, width), lambda j: (0, j, 0, 0))],
        out_specs=pl.BlockSpec((NZ // 2, BLK, 2 * width), lambda j: (j, 0, 0)),
        out_shape=jax.ShapeDtypeStruct((NZ, BLK, 2 * width), BF16),
        name="sum_for_z",
        **params_of(8 * NZ * BLK * width, 20 * NZ * BLK * width),
    )(*over_x, over_y)


def body(acts, cotangent, master, moment, second):
    x, c, y = (lax.axis_index(a) for a in ("x", "c", "y"))
    idx = jnp.stack([c, x, y]).astype(jnp.int32)
    theirs_c = product(acts, cotangent, idx, 0, FLOW_C)
    got_c = shift(theirs_c, "c", NC, 1)
    theirs_b = product(acts, cotangent, idx, FLOW_C, FLOW_B)
    got_b = shift(theirs_b, "c", NC, 1)
    over_y = exchange(product_for_y(acts, cotangent, got_c, idx, 0), "y", NY, (1, 3, 2))
    over_x = swap(product_for_x(acts, cotangent, got_b, idx, FLOW_C, FLOW_B), "x")
    over_yx = exchange(sum_for_x(over_y, idx), "x", NX, (1, 3, 2))
    over_xy = swap(sum_for_y(over_x), "y")
    rows = sum_for_z(over_yx, over_xy).reshape(NZ * NC * NY, BLK // NC // NY, 2 * TN)
    pieces = swap(rows, ("z", "c", "y")).reshape(NZ, NC * NY, BLK // NC // NY, 2 * TN)
    pieces = jnp.sum(pieces.astype(F32), axis=0)
    grad = jnp.concatenate(
        [pieces[h * NY + k, :, f * TN : (f + 1) * TN] for h in range(NC) for f in range(2) for k in range(NY)], axis=-1
    )
    new_moment = 0.9 * moment + 0.1 * grad
    new_second = 0.95 * second + 0.05 * grad * grad
    corr_one = 1.0 - 0.9**10
    corr_two = 1.0 - 0.95**10
    update = new_moment / corr_one / (jnp.sqrt(new_second / corr_two) + 1e-08)
    new_master = master - 0.02 * (update + 0.1 * master)
    every = exchange([new_master.astype(BF16)] * NY, "y", NY, (1, 2, 3))
    params = jnp.concatenate([lax.select_n(lax.rem(y - k + NY, NY), *every) for k in range(NY)], axis=0)
    return (new_master, new_moment, new_second, params)


def solution(mesh):
    fine = Mesh(mesh.devices.reshape(NZ, NX, NC, NY), ("z", "x", "c", "y"))
    split = P(("z", "x", "c", "y"), None)
    return jax.shard_map(
        body,
        mesh=fine,
        in_specs=(split,) * 5,
        out_specs=(split, split, split, P(("z", "x", "c"), None)),
        check_vma=False,
    )
```

```python
import jax
import jax.numpy as jnp
from jax import lax
from jax.experimental import pallas as pl
from jax.experimental.pallas import tpu as pltpu
from jax.sharding import Mesh, PartitionSpec as P

NZ, NX, NC, NY = 8, 4, 2, 4
D, FFW = 1536, 4096
HALF = FFW // 2
TN = 256
BLK = D // (NZ * NX)
FLOW_C = 1024
FLOW_B = 1024
T = 1024
F32, BF16 = jnp.float32, jnp.bfloat16
VMEM_LIMIT = 40 * 1024 * 1024
DN = (((0,), (0,)), ((), ()))


def params_of(flops, nbytes):
    return dict(
        compiler_params=pltpu.CompilerParams(vmem_limit_bytes=VMEM_LIMIT),
        cost_estimate=pl.CostEstimate(flops=flops, bytes_accessed=nbytes, transcendentals=0),
    )


def shift(v, axis, n, s):
    return lax.ppermute(v, axis, [(i, (i + s) % n) for i in range(n)])


def exchange(pieces, axis, n, order):
    return [pieces[0]] + [shift(pieces[s], axis, n, s) for s in order]


def swap(v, axes):
    return lax.all_to_all(v, axes, 0, 0, tiled=True)


def product_mine(acts, cot, idx, base, ncols):
    tn = 2 * TN

    def kernel(idx_ref, a, c, o):
        o[...] = lax.dot_general(a[...], c[...], DN, preferred_element_type=F32).astype(BF16)

    return pl.pallas_call(
        kernel,
        grid_spec=pltpu.PrefetchScalarGridSpec(
            num_scalar_prefetch=1,
            grid=(ncols // tn,),
            in_specs=[
                pl.BlockSpec((T, D), lambda j, s: (0, 0)),
                pl.BlockSpec((T, tn), lambda j, s: (0, s[0] * (HALF // tn) + base // tn + j)),
            ],
            out_specs=pl.BlockSpec((D, tn), lambda j, s: (0, j)),
        ),
        out_shape=jax.ShapeDtypeStruct((D, ncols), BF16),
        name="product_mine",
        **params_of(2 * T * D * ncols, 2 * (T * D + T * ncols + D * ncols)),
    )(idx, acts, cot)


def product_for_x(acts, cot, mine, ncols):
    def kernel(a, c, m, o):
        acc = lax.dot_general(a[...], c[...], DN, preferred_element_type=F32) + m[...].astype(F32)
        acc = acc.astype(BF16).reshape(NZ, NX, BLK, TN)
        for x in range(NX):
            o[x] = acc[:, x]

    return pl.pallas_call(
        kernel,
        grid=(ncols // TN,),
        in_specs=[
            pl.BlockSpec((T, D), lambda j: (0, 0)),
            pl.BlockSpec((T, TN), lambda j: (0, j)),
            pl.BlockSpec((D, TN), lambda j: (0, j)),
        ],
        out_specs=pl.BlockSpec((NX, NZ, BLK, TN), lambda j: (0, 0, 0, j)),
        out_shape=jax.ShapeDtypeStruct((NX, NZ, BLK, ncols), BF16),
        name="product_for_x",
        **params_of(2 * T * D * ncols, 2 * (T * D + T * ncols + 2 * D * ncols)),
    )(acts, cot, mine)


def product_for_y(acts, cot, acts_other, cot_other, idx, base):
    def kernel(idx_ref, a, c, a2, c2, *outs):
        acc = lax.dot_general(a[...], c[...], DN, preferred_element_type=F32)
        acc = acc + lax.dot_general(a2[...], c2[...], DN, preferred_element_type=F32)
        for o in range(NY):

            @pl.when(pl.program_id(0) == o)
            def _():
                outs[o][...] = acc.astype(BF16)

    return pl.pallas_call(
        kernel,
        grid_spec=pltpu.PrefetchScalarGridSpec(
            num_scalar_prefetch=1,
            grid=(NY,),
            in_specs=[
                pl.BlockSpec((T, D), lambda j, s: (0, 0)),
                pl.BlockSpec((T, TN), lambda j, s: (0, s[0] * (HALF // TN) + base // TN + lax.rem(s[2] + j, NY))),
                pl.BlockSpec((T, D), lambda j, s: (0, 0)),
                pl.BlockSpec((T, TN), lambda j, s: (0, lax.rem(s[2] + j, NY))),
            ],
            out_specs=[pl.BlockSpec((D, TN), lambda j, s: (0, 0))] * NY,
        ),
        out_shape=[jax.ShapeDtypeStruct((D, TN), BF16)] * NY,
        name="product_for_y",
        **params_of(4 * T * D * TN * NY, 2 * (2 * T * D + 2 * T * TN * NY + D * TN * NY)),
    )(idx, acts, cot, acts_other, cot_other)


def sum_for_x(parts, idx):
    width = parts[0].shape[-1]

    def kernel(idx_ref, *refs):
        ins, outs = refs[:NY], refs[NY:]
        for o in range(NX):
            x = lax.rem(idx_ref[1] + o, NX)
            for z in range(NZ):
                total = ins[0][z, x].astype(F32)
                for r in ins[1:]:
                    total = total + r[z, x].astype(F32)
                outs[o][z] = total.astype(BF16)

    return pl.pallas_call(
        kernel,
        grid_spec=pltpu.PrefetchScalarGridSpec(
            num_scalar_prefetch=1,
            grid=(1,),
            in_specs=[pl.BlockSpec((NZ, NX, BLK, width), lambda j, s: (0, 0, 0, 0))] * NY,
            out_specs=[pl.BlockSpec((NZ, BLK, width), lambda j, s: (0, 0, 0))] * NX,
        ),
        out_shape=[jax.ShapeDtypeStruct((NZ, BLK, width), BF16)] * NX,
        name="sum_for_x",
        **params_of(4 * D * width, 2 * 5 * D * width),
    )(idx, *[p.reshape(NZ, NX, BLK, width) for p in parts])


def sum_for_y(over_x):
    width = over_x.shape[-1] // NY

    def kernel(r, o):
        total = r[0].astype(F32)
        for k in range(1, NX):
            total = total + r[k].astype(F32)
        o[0] = total.astype(BF16)

    return pl.pallas_call(
        kernel,
        grid=(NY,),
        in_specs=[pl.BlockSpec((NX, NZ, BLK, width), lambda j: (0, 0, 0, j))],
        out_specs=pl.BlockSpec((1, NZ, BLK, width), lambda j: (j, 0, 0, 0)),
        out_shape=jax.ShapeDtypeStruct((NY, NZ, BLK, width), BF16),
        name="sum_for_y",
        **params_of(4 * D * width, 2 * 5 * D * width),
    )(over_x)


def sum_for_z(over_x, over_y):
    width = over_y.shape[-1]

    def kernel(*refs):
        ins, r, o = refs[:NX], refs[NX], refs[NX + 1]
        total = ins[0][...].astype(F32)
        for p in ins[1:]:
            total = total + p[...].astype(F32)
        o[:, :, :width] = total.astype(BF16)
        total = r[0].astype(F32)
        for k in range(1, NY):
            total = total + r[k].astype(F32)
        o[:, :, width:] = total.astype(BF16)

    spec = pl.BlockSpec((NZ // 2, BLK, width), lambda j: (j, 0, 0))
    return pl.pallas_call(
        kernel,
        grid=(2,),
        in_specs=[spec] * NX + [pl.BlockSpec((NY, NZ // 2, BLK, width), lambda j: (0, j, 0, 0))],
        out_specs=pl.BlockSpec((NZ // 2, BLK, 2 * width), lambda j: (j, 0, 0)),
        out_shape=jax.ShapeDtypeStruct((NZ, BLK, 2 * width), BF16),
        name="sum_for_z",
        **params_of(8 * NZ * BLK * width, 20 * NZ * BLK * width),
    )(*over_x, over_y)


def body(acts, cotangent, master, moment, second):
    x, c, y = (lax.axis_index(a) for a in ("x", "c", "y"))
    idx = jnp.stack([c, x, y]).astype(jnp.int32)
    acts_other = shift(acts, "c", NC, 1)
    columns = lambda base, n: lax.dynamic_slice_in_dim(cotangent, (1 - c) * HALF + base, n, 1)
    other_b = shift(columns(FLOW_C, FLOW_B), "c", NC, 1)
    other_c = shift(columns(0, FLOW_C), "c", NC, 1)
    mine_b = product_mine(acts, cotangent, idx, FLOW_C, FLOW_B)
    over_x = swap(product_for_x(acts_other, other_b, mine_b, FLOW_B), "x")
    over_y = exchange(product_for_y(acts, cotangent, acts_other, other_c, idx, 0), "y", NY, (1, 3, 2))
    over_yx = exchange(sum_for_x(over_y, idx), "x", NX, (1, 3, 2))
    over_xy = swap(sum_for_y(over_x), "y")
    rows = sum_for_z(over_yx, over_xy).reshape(NZ * NC * NY, BLK // NC // NY, 2 * TN)
    pieces = swap(rows, ("z", "c", "y")).reshape(NZ, NC * NY, BLK // NC // NY, 2 * TN)
    pieces = jnp.sum(pieces.astype(F32), axis=0)
    grad = jnp.concatenate(
        [pieces[h * NY + k, :, f * TN : (f + 1) * TN] for h in range(NC) for f in range(2) for k in range(NY)], axis=-1
    )
    new_moment = 0.9 * moment + 0.1 * grad
    new_second = 0.95 * second + 0.05 * grad * grad
    corr_one = 1.0 - 0.9**10
    corr_two = 1.0 - 0.95**10
    update = new_moment / corr_one / (jnp.sqrt(new_second / corr_two) + 1e-08)
    new_master = master - 0.02 * (update + 0.1 * master)
    every = exchange([new_master.astype(BF16)] * NY, "y", NY, (1, 2, 3))
    params = jnp.concatenate([lax.select_n(lax.rem(y - k + NY, NY), *every) for k in range(NY)], axis=0)
    return (new_master, new_moment, new_second, params)


def solution(mesh):
    fine = Mesh(mesh.devices.reshape(NZ, NX, NC, NY), ("z", "x", "c", "y"))
    split = P(("z", "x", "c", "y"), None)
    return jax.shard_map(
        body,
        mesh=fine,
        in_specs=(split,) * 5,
        out_specs=(split, split, split, P(("z", "x", "c"), None)),
        check_vma=False,
    )
```

```python
import jax
import jax.numpy as jnp
from jax import lax
from jax.experimental import pallas as pl
from jax.experimental.pallas import tpu as pltpu
from jax.sharding import Mesh, PartitionSpec as P

NZ, NX, NC, NY = 8, 4, 2, 4
D, FFW = 1536, 4096
HALF = FFW // 2
TN = 256
BLK = D // (NZ * NX)
OWN = BLK // NC // NY
FLOW_C = 1024
FLOW_B = 1024
T = 1024
F32, BF16 = jnp.float32, jnp.bfloat16
ORDER = (1, 3, 2)
VMEM_LIMIT = 40 * 1024 * 1024
DN = (((0,), (0,)), ((), ()))
WHOLE = pl.BlockSpec(memory_space=pltpu.VMEM)


def params_of(flops, nbytes):
    return dict(
        compiler_params=pltpu.CompilerParams(vmem_limit_bytes=VMEM_LIMIT),
        cost_estimate=pl.CostEstimate(flops=flops, bytes_accessed=nbytes, transcendentals=0),
    )


def shift(v, axis, n, s):
    return lax.ppermute(v, axis, [(i, (i + s) % n) for i in range(n)])


def exchange(pieces, axis, n, order):
    return [pieces[0]] + [shift(pieces[s], axis, n, s) for s in order]


def swap(v, axes):
    return lax.all_to_all(v, axes, 0, 0, tiled=True)


def product(acts, cot, idx, base, ncols):
    tn = 2 * TN

    def kernel(idx_ref, a, c, o):
        o[...] = lax.dot_general(a[...], c[...], DN, preferred_element_type=F32).astype(BF16)

    return pl.pallas_call(
        kernel,
        grid_spec=pltpu.PrefetchScalarGridSpec(
            num_scalar_prefetch=1,
            grid=(ncols // tn,),
            in_specs=[
                WHOLE,
                pl.BlockSpec((T, tn), lambda j, s: (0, (1 - s[0]) * (HALF // tn) + base // tn + j)),
            ],
            out_specs=pl.BlockSpec((D, tn), lambda j, s: (0, j)),
        ),
        out_shape=jax.ShapeDtypeStruct((D, ncols), BF16),
        name="product_theirs",
        **params_of(2 * T * D * ncols, 2 * (T * D + T * ncols + D * ncols)),
    )(idx, acts, cot)


def ahead(idx_ref, axis, o):
    return lax.rem(idx_ref["cxy".index(axis)] + o, 4)


def product_for_y(acts, cot, got, idx, base):
    def kernel(idx_ref, a, c, r, *outs):
        acc = lax.dot_general(a[...], c[...], DN, preferred_element_type=F32) + r[...].astype(F32)
        acc = acc.astype(BF16).reshape(NZ * NX, BLK, TN)
        for o in range(NY):

            @pl.when(pl.program_id(0) == o)
            def _():
                for out, here, there in parts_of(o, NZ * NX // 2):
                    outs[out][there] = acc[here]

    place = lambda j, s: lax.rem(s[2] + j, NY)
    shapes = ring_shapes(NZ * NX, TN)
    return pl.pallas_call(
        kernel,
        grid_spec=pltpu.PrefetchScalarGridSpec(
            num_scalar_prefetch=1,
            grid=(NY,),
            in_specs=[
                WHOLE,
                pl.BlockSpec((T, TN), lambda j, s: (0, s[0] * (HALF // TN) + base // TN + place(j, s))),
                pl.BlockSpec((D, TN), lambda j, s: (0, place(j, s))),
            ],
            out_specs=[pl.BlockSpec(o.shape, lambda j, s: (0, 0, 0)) for o in shapes],
        ),
        out_shape=shapes,
        name="product_for_y",
        **params_of(2 * T * D * TN * NY, 2 * (T * D + T * TN * NY + 2 * D * TN * NY)),
    )(idx, acts, cot, got)


def product_for_x(acts, cot, got, idx, base, ncols):
    tn = 2 * TN

    def kernel(idx_ref, a, c, r, *rest):
        outs, acc = rest[:-1], rest[-1]
        acc[...] = lax.dot_general(a[...], c[...], DN, preferred_element_type=F32) + r[...].astype(F32)
        for o in range(NX):
            x = ahead(idx_ref, "x", o)
            for out, here, there in parts_of(o, NZ // 2):
                for z in range(here.start, here.stop):
                    rows = pl.ds(pl.multiple_of((z * NX + x) * BLK, BLK), BLK)
                    outs[out][z - here.start + there.start] = acc[rows, :].astype(BF16)

    shapes = ring_shapes(NZ, ncols)
    return pl.pallas_call(
        kernel,
        grid_spec=pltpu.PrefetchScalarGridSpec(
            num_scalar_prefetch=1,
            grid=(ncols // tn,),
            in_specs=[
                WHOLE,
                pl.BlockSpec((T, tn), lambda j, s: (0, s[0] * (HALF // tn) + base // tn + j)),
                pl.BlockSpec((D, tn), lambda j, s: (0, j)),
            ],
            out_specs=[pl.BlockSpec(o.shape[:2] + (tn,), lambda j, s: (0, 0, j)) for o in shapes],
            scratch_shapes=[pltpu.VMEM((D, tn), F32)],
        ),
        out_shape=shapes,
        name="product_for_x",
        **params_of(2 * T * D * ncols, 2 * (T * D + T * ncols + 2 * D * ncols)),
    )(idx, acts, cot, got)


def ring_shapes(n, width):
    return [jax.ShapeDtypeStruct((k, BLK, width), BF16) for k in (n, n, n, n // 2, n // 2)]


def parts_of(o, half):
    upper, lower = slice(0, half), slice(half, 2 * half)
    return {
        0: ((0, upper, upper), (0, lower, lower)),
        1: ((3, upper, upper), (1, lower, lower)),
        2: ((1, upper, upper), (2, lower, lower)),
        3: ((2, upper, upper), (4, lower, upper)),
    }[o]


def pass_on(keep_up, keep_down, from_down, from_up):
    half = keep_up.shape[0]

    def kernel(ku, kd, fd, fu, up, down):
        for k in range(half):
            up[k] = (ku[k].astype(F32) + fd[k].astype(F32)).astype(BF16)
            down[k] = (kd[k].astype(F32) + fu[half + k].astype(F32)).astype(BF16)

    return pl.pallas_call(
        kernel,
        in_specs=[WHOLE] * 4,
        out_specs=[WHOLE] * 2,
        out_shape=[jax.ShapeDtypeStruct(keep_up.shape, BF16)] * 2,
        name="pass_on",
        **params_of(2 * keep_up.size, 12 * keep_up.size),
    )(keep_up, keep_down, from_down, from_up)


def ring(pieces, axis):
    own, up, down, keep_up, keep_down = pieces
    from_down, from_up = shift(up, axis, 4, 1), shift(down, axis, 4, 3)
    up, down = pass_on(keep_up, keep_down, from_down, from_up)
    return own, from_down, from_up, shift(up, axis, 4, 1), shift(down, axis, 4, 3)


def total_of(refs, z):
    total = refs[0][z].astype(F32)
    for r in refs[1:]:
        total = total + r[z].astype(F32)
    return total


def sum_and_cut(arrived, idx, axis):
    n = arrived[0].shape[0]

    def kernel(idx_ref, own, from_down, from_up, up, down, *outs):
        for o in range(4):
            t = ahead(idx_ref, axis, o)
            for z in range(NZ):
                if axis == "x":
                    place, rest = z * NX + t, slice(None)
                else:
                    place, rest = z, pl.ds(pl.multiple_of(t * TN, TN), TN)
                total = own[place, :, rest].astype(F32)
                if z < NZ // 2:
                    total = total + from_up[place, :, rest].astype(F32) + up[place, :, rest].astype(F32)
                else:
                    total = total + from_down[place, :, rest].astype(F32) + down[place - n // 2, :, rest].astype(F32)
                outs[o][z] = total.astype(BF16)

    return pl.pallas_call(
        kernel,
        grid_spec=pltpu.PrefetchScalarGridSpec(
            num_scalar_prefetch=1, grid=(1,), in_specs=[WHOLE] * 5, out_specs=[WHOLE] * 4
        ),
        out_shape=[jax.ShapeDtypeStruct((NZ, BLK, TN), BF16)] * 4,
        name="sum_for_" + axis,
        **params_of(4 * D * TN, 10 * D * TN),
    )(idx, *arrived)


def sum_for_z(flows):
    counts = [len(f) for f in flows]

    def kernel(*refs):
        ins, o = refs[:-1], refs[-1]
        for z in range(NZ):
            totals = [total_of(ins[: counts[0]], z), total_of(ins[counts[0] :], z)]
            for y in range(NY):
                rows = [t[h * NY * OWN + y * OWN : h * NY * OWN + (y + 1) * OWN] for t in totals for h in range(NC)]
                o[z * NY + y] = jnp.concatenate(rows, axis=0).astype(BF16)

    return pl.pallas_call(
        kernel,
        in_specs=[WHOLE] * sum(counts),
        out_specs=WHOLE,
        out_shape=jax.ShapeDtypeStruct((NZ * NY, 2 * NC * OWN, TN), BF16),
        name="sum_for_z",
        **params_of(8 * D * TN, 20 * D * TN),
    )(*flows[0], *flows[1])


def settle(flows, c):
    pieces = swap(sum_for_z(flows), ("z", "y")).astype(F32)
    pieces = jnp.sum(pieces.reshape(NZ, NY, 2, NC, OWN, TN), axis=0)
    mine, theirs = [
        lax.select_n(c == h, pieces[:, :, 1], pieces[:, :, 0]).astype(BF16) for h in (0, 1)
    ]
    got = shift(theirs, "c", NC, 1)
    halves = [lax.select_n(c == h, got, mine) for h in range(NC)]
    return jnp.concatenate([p[k, f] for p in halves for f in range(2) for k in range(NY)], axis=-1).astype(F32)


def body(acts, cotangent, master, moment, second):
    x, c, y = (lax.axis_index(a) for a in ("x", "c", "y"))
    idx = jnp.stack([c, x, y]).astype(jnp.int32)
    theirs_c = product(acts, cotangent, idx, 0, FLOW_C)
    got_c = shift(theirs_c, "c", NC, 1)
    theirs_b = product(acts, cotangent, idx, FLOW_C, FLOW_B)
    got_b = shift(theirs_b, "c", NC, 1)
    over_x = ring(product_for_x(acts, cotangent, got_b, idx, FLOW_C, FLOW_B), "x")
    over_y = ring(product_for_y(acts, cotangent, got_c, idx, 0), "y")
    over_xy = exchange(sum_and_cut(over_x, idx, "y"), "y", 4, ORDER)
    over_yx = exchange(sum_and_cut(over_y, idx, "x"), "x", 4, ORDER)
    grad = settle((over_yx, over_xy), c)
    new_moment = 0.9 * moment + 0.1 * grad
    new_second = 0.95 * second + 0.05 * grad * grad
    corr_one = 1.0 - 0.9**10
    corr_two = 1.0 - 0.95**10
    update = new_moment / corr_one / (jnp.sqrt(new_second / corr_two) + 1e-08)
    new_master = master - 0.02 * (update + 0.1 * master)
    every = exchange([new_master.astype(BF16)] * NY, "y", NY, (1, 2, 3))
    params = jnp.concatenate([lax.select_n(lax.rem(y - k + NY, NY), *every) for k in range(NY)], axis=0)
    return (new_master, new_moment, new_second, params)


def solution(mesh):
    fine = Mesh(mesh.devices.reshape(NZ, NX, NC, NY), ("z", "x", "c", "y"))
    split = P(("z", "x", "c", "y"), None)
    return jax.shard_map(
        body,
        mesh=fine,
        in_specs=(split,) * 5,
        out_specs=(split, split, split, P(("z", "x", "c"), None)),
        check_vma=False,
    )
```

```python
import jax
import jax.numpy as jnp
from jax import lax
from jax.experimental import pallas as pl
from jax.experimental.pallas import tpu as pltpu
from jax.sharding import Mesh, PartitionSpec as P

NZ, NX, NC, NY = 8, 4, 2, 4
D, FFW = 1536, 4096
HALF = FFW // 2
TN = 256
BLK = D // (NZ * NX)
OWN = BLK // NC // NY
FLOW_C = 1024
FLOW_B = 1024
T = 1024
F32, BF16 = jnp.float32, jnp.bfloat16
ORDER = (1, 3, 2)
VMEM_LIMIT = 40 * 1024 * 1024
DN = (((0,), (0,)), ((), ()))
WHOLE = pl.BlockSpec(memory_space=pltpu.VMEM)


def params_of(flops, nbytes):
    return dict(
        compiler_params=pltpu.CompilerParams(vmem_limit_bytes=VMEM_LIMIT),
        cost_estimate=pl.CostEstimate(flops=flops, bytes_accessed=nbytes, transcendentals=0),
    )


def shift(v, axis, n, s):
    return lax.ppermute(v, axis, [(i, (i + s) % n) for i in range(n)])


def exchange(pieces, axis, n, order):
    return [pieces[0]] + [shift(pieces[s], axis, n, s) for s in order]


def swap(v, axes):
    return lax.all_to_all(v, axes, 0, 0, tiled=True)


def product(acts, cot, idx, base, ncols, after=()):
    tn = 2 * TN

    def kernel(idx_ref, a, c, *rest):
        rest[-1][...] = lax.dot_general(a[...], c[...], DN, preferred_element_type=F32).astype(BF16)

    return pl.pallas_call(
        kernel,
        grid_spec=pltpu.PrefetchScalarGridSpec(
            num_scalar_prefetch=1,
            grid=(ncols // tn,),
            in_specs=[
                WHOLE,
                pl.BlockSpec((T, tn), lambda j, s: (0, (1 - s[0]) * (HALF // tn) + base // tn + j)),
            ]
            + [pl.BlockSpec(memory_space=pl.ANY)] * len(after),
            out_specs=pl.BlockSpec((D, tn), lambda j, s: (0, j)),
        ),
        out_shape=jax.ShapeDtypeStruct((D, ncols), BF16),
        name="product_theirs",
        **params_of(2 * T * D * ncols, 2 * (T * D + T * ncols + D * ncols)),
    )(idx, acts, cot, *after)


def ahead(idx_ref, axis, o):
    return lax.rem(idx_ref["cxy".index(axis)] + o, 4)


def product_for_y(acts, cot, got, idx, base, part, after=()):
    half = D // 2
    upper, lower = slice(0, half), slice(half, D)
    full, one_upper, one_lower = (2, 3, 1) if part == 0 else (0, 1, 3)
    full_lower = 1 if part == 0 else 0
    one_lower_out = 0 if part == 0 else 1

    def kernel(idx_ref, a, c_full, c_upper, c_lower, r, *rest):
        outs = rest[-2:]

        def add(product, rows, o):
            columns = pl.ds(pl.multiple_of(lax.rem(idx_ref[2] + o, NY) * TN, TN), TN)
            return (product + r[rows, columns].astype(F32)).astype(BF16)

        product = lax.dot_general(a[...], c_full[...], DN, preferred_element_type=F32)
        outs[0][upper, :] = add(product[upper], upper, full)
        outs[full_lower][lower, :] = add(product[lower], lower, full)
        product = lax.dot_general(a[:, upper], c_upper[...], DN, preferred_element_type=F32)
        outs[1][upper, :] = add(product, upper, one_upper)
        product = lax.dot_general(a[:, lower], c_lower[...], DN, preferred_element_type=F32)
        outs[one_lower_out][lower, :] = add(product, lower, one_lower)

    def columns(o):
        place = lambda j, s: (0, s[0] * (HALF // TN) + base // TN + lax.rem(s[2] + o, NY))
        return pl.BlockSpec((T, TN), place)

    return pl.pallas_call(
        kernel,
        grid_spec=pltpu.PrefetchScalarGridSpec(
            num_scalar_prefetch=1,
            grid=(1,),
            in_specs=[WHOLE]
            + [columns(o) for o in (full, one_upper, one_lower)]
            + [WHOLE]
            + [pl.BlockSpec(memory_space=pl.ANY)] * len(after),
            out_specs=[WHOLE] * 2,
        ),
        out_shape=[jax.ShapeDtypeStruct((D, TN), BF16)] * 2,
        name="product_for_y",
        **params_of(4 * T * D * TN, 2 * (T * D + 4 * T * TN + 4 * D * TN)),
    )(idx, acts, cot, cot, cot, got, *after)


def product_for_x(acts, cot, got, idx, base, ncols, after):
    tn = 2 * TN

    def kernel(idx_ref, a, c, r, _, *rest):
        outs, acc = rest[:-1], rest[-1]
        acc[...] = lax.dot_general(a[...], c[...], DN, preferred_element_type=F32) + r[...].astype(F32)
        for o in range(NX):
            x = ahead(idx_ref, "x", o)
            for out, half in parts_of(o, NZ // 2):
                for z in range(half.start, half.stop):
                    rows = pl.ds(pl.multiple_of((z * NX + x) * BLK, BLK), BLK)
                    outs[out][z] = acc[rows, :].astype(BF16)

    shapes = [jax.ShapeDtypeStruct((NZ, BLK, ncols), BF16)] * 4
    return pl.pallas_call(
        kernel,
        grid_spec=pltpu.PrefetchScalarGridSpec(
            num_scalar_prefetch=1,
            grid=(ncols // tn,),
            in_specs=[
                WHOLE,
                pl.BlockSpec((T, tn), lambda j, s: (0, s[0] * (HALF // tn) + base // tn + j)),
                pl.BlockSpec((D, tn), lambda j, s: (0, j)),
                pl.BlockSpec(memory_space=pl.ANY),
            ],
            out_specs=[pl.BlockSpec(o.shape[:2] + (tn,), lambda j, s: (0, 0, j)) for o in shapes],
            scratch_shapes=[pltpu.VMEM((D, tn), F32)],
        ),
        out_shape=shapes,
        name="product_for_x",
        **params_of(2 * T * D * ncols, 2 * (T * D + T * ncols + 2 * D * ncols)),
    )(idx, acts, cot, got, after)


def parts_of(o, half):
    upper, lower = slice(0, half), slice(half, 2 * half)
    arrays = ((0, 0), (3, 1), (1, 2), (2, 3))[o]
    return ((arrays[0], upper), (arrays[1], lower))


def pass_on(keep, from_down, from_up):
    half = keep.shape[0] // 2

    def kernel(k, fd, fu, up, down):
        for n in range(half):
            up[n] = (k[n].astype(F32) + fd[n].astype(F32)).astype(BF16)
            down[n] = (k[half + n].astype(F32) + fu[half + n].astype(F32)).astype(BF16)

    return pl.pallas_call(
        kernel,
        in_specs=[WHOLE] * 3,
        out_specs=[WHOLE] * 2,
        out_shape=[jax.ShapeDtypeStruct((half,) + keep.shape[1:], BF16)] * 2,
        name="pass_on",
        **params_of(keep.size, 6 * keep.size),
    )(keep, from_down, from_up)


def ring(up, down, axis):
    return shift(up, axis, 4, 1), shift(down, axis, 4, 3)


def ring_end(own, keep, from_down, from_up, axis):
    up, down = pass_on(keep, from_down, from_up)
    return own, from_down, from_up, shift(up, axis, 4, 1), shift(down, axis, 4, 3)


def total_of(refs, z):
    total = refs[0][z].astype(F32)
    for r in refs[1:]:
        total = total + r[z].astype(F32)
    return total


def sum_and_cut(arrived, idx, axis):
    n = arrived[0].shape[0]

    def kernel(idx_ref, own, from_down, from_up, up, down, *outs):
        for o in range(4):
            t = ahead(idx_ref, axis, o)
            for z in range(NZ):
                if axis == "x":
                    place, rest = z * NX + t, slice(None)
                else:
                    place, rest = z, pl.ds(pl.multiple_of(t * TN, TN), TN)
                total = own[place, :, rest].astype(F32)
                if z < NZ // 2:
                    total = total + from_up[place, :, rest].astype(F32) + up[place, :, rest].astype(F32)
                else:
                    total = total + from_down[place, :, rest].astype(F32) + down[place - n // 2, :, rest].astype(F32)
                outs[o][z] = total.astype(BF16)

    return pl.pallas_call(
        kernel,
        grid_spec=pltpu.PrefetchScalarGridSpec(
            num_scalar_prefetch=1, grid=(1,), in_specs=[WHOLE] * 5, out_specs=[WHOLE] * 4
        ),
        out_shape=[jax.ShapeDtypeStruct((NZ, BLK, TN), BF16)] * 4,
        name="sum_for_" + axis,
        **params_of(4 * D * TN, 10 * D * TN),
    )(idx, *arrived)


def sum_for_z(flows):
    counts = [len(f) for f in flows]

    def kernel(*refs):
        ins, o = refs[:-1], refs[-1]
        for z in range(NZ):
            totals = [total_of(ins[: counts[0]], z), total_of(ins[counts[0] :], z)]
            for y in range(NY):
                rows = [t[h * NY * OWN + y * OWN : h * NY * OWN + (y + 1) * OWN] for t in totals for h in range(NC)]
                o[z * NY + y] = jnp.concatenate(rows, axis=0).astype(BF16)

    return pl.pallas_call(
        kernel,
        in_specs=[WHOLE] * sum(counts),
        out_specs=WHOLE,
        out_shape=jax.ShapeDtypeStruct((NZ * NY, 2 * NC * OWN, TN), BF16),
        name="sum_for_z",
        **params_of(8 * D * TN, 20 * D * TN),
    )(*flows[0], *flows[1])


def settle(flows, c):
    pieces = swap(sum_for_z(flows), ("z", "y")).astype(F32)
    pieces = jnp.sum(pieces.reshape(NZ, NY, 2, NC, OWN, TN), axis=0)
    mine, theirs = [
        lax.select_n(c == h, pieces[:, :, 1], pieces[:, :, 0]).astype(BF16) for h in (0, 1)
    ]
    got = shift(theirs, "c", NC, 1)
    halves = [lax.select_n(c == h, got, mine) for h in range(NC)]
    return jnp.concatenate([p[k, f] for p in halves for f in range(2) for k in range(NY)], axis=-1).astype(F32)


def body(acts, cotangent, master, moment, second):
    x, c, y = (lax.axis_index(a) for a in ("x", "c", "y"))
    idx = jnp.stack([c, x, y]).astype(jnp.int32)
    blocks = lambda p: p.reshape(NZ * NX, BLK, TN)
    theirs_c = product(acts, cotangent, idx, 0, FLOW_C)
    got_c = shift(theirs_c, "c", NC, 1)
    theirs_b = product(acts, cotangent, idx, FLOW_C, FLOW_B, (theirs_c,))
    got_b = shift(theirs_b, "c", NC, 1)
    up, down = product_for_y(acts, cotangent, got_c, idx, 0, 0)
    first_y = ring(blocks(up), blocks(down), "y")
    own_b, up_b, down_b, keep_b = product_for_x(acts, cotangent, got_b, idx, FLOW_C, FLOW_B, up)
    first_x = ring(up_b, down_b, "x")
    own, keep = product_for_y(acts, cotangent, got_c, idx, 0, 1, (own_b,))
    over_y = ring_end(blocks(own), blocks(keep), *first_y, "y")
    over_x = ring_end(own_b, keep_b, *first_x, "x")
    over_xy = exchange(sum_and_cut(over_x, idx, "y"), "y", 4, ORDER)
    over_yx = exchange(sum_and_cut(over_y, idx, "x"), "x", 4, ORDER)
    grad = settle((over_yx, over_xy), c)
    new_moment = 0.9 * moment + 0.1 * grad
    new_second = 0.95 * second + 0.05 * grad * grad
    corr_one = 1.0 - 0.9**10
    corr_two = 1.0 - 0.95**10
    update = new_moment / corr_one / (jnp.sqrt(new_second / corr_two) + 1e-08)
    new_master = master - 0.02 * (update + 0.1 * master)
    every = exchange([new_master.astype(BF16)] * NY, "y", NY, (1, 2, 3))
    params = jnp.concatenate([lax.select_n(lax.rem(y - k + NY, NY), *every) for k in range(NY)], axis=0)
    return (new_master, new_moment, new_second, params)


def solution(mesh):
    fine = Mesh(mesh.devices.reshape(NZ, NX, NC, NY), ("z", "x", "c", "y"))
    split = P(("z", "x", "c", "y"), None)
    return jax.shard_map(
        body,
        mesh=fine,
        in_specs=(split,) * 5,
        out_specs=(split, split, split, P(("z", "x", "c"), None)),
        check_vma=False,
    )
```

```python
import jax
import jax.numpy as jnp
from jax import lax
from jax.experimental import pallas as pl
from jax.experimental.pallas import tpu as pltpu
from jax.sharding import Mesh, PartitionSpec as P

NZ, NX, NC, NY = 8, 4, 2, 4
D, FFW = 1536, 4096
HALF = FFW // 2
TN = 256
BLK = D // (NZ * NX)
OWN = BLK // NC // NY
FLOW_C = 1024
FLOW_B = 1024
T = 1024
F32, BF16 = jnp.float32, jnp.bfloat16
ORDER = (1, 3, 2)
VMEM_LIMIT = 40 * 1024 * 1024
DN = (((0,), (0,)), ((), ()))
WHOLE = pl.BlockSpec(memory_space=pltpu.VMEM)


def params_of(flops, nbytes):
    return dict(
        compiler_params=pltpu.CompilerParams(vmem_limit_bytes=VMEM_LIMIT),
        cost_estimate=pl.CostEstimate(flops=flops, bytes_accessed=nbytes, transcendentals=0),
    )


def shift(v, axis, n, s):
    return lax.ppermute(v, axis, [(i, (i + s) % n) for i in range(n)])


def exchange(pieces, axis, n, order):
    return [pieces[0]] + [shift(pieces[s], axis, n, s) for s in order]


def swap(v, axes):
    return lax.all_to_all(v, axes, 0, 0, tiled=True)


def product(acts, cot, idx, base, ncols, after=()):
    tn = 2 * TN

    def kernel(idx_ref, a, c, *rest):
        rest[-1][...] = lax.dot_general(a[...], c[...], DN, preferred_element_type=F32).astype(BF16)

    return pl.pallas_call(
        kernel,
        grid_spec=pltpu.PrefetchScalarGridSpec(
            num_scalar_prefetch=1,
            grid=(ncols // tn,),
            in_specs=[
                WHOLE,
                pl.BlockSpec((T, tn), lambda j, s: (0, (1 - s[0]) * (HALF // tn) + base // tn + j)),
            ]
            + [pl.BlockSpec(memory_space=pl.ANY)] * len(after),
            out_specs=pl.BlockSpec((D, tn), lambda j, s: (0, j)),
        ),
        out_shape=jax.ShapeDtypeStruct((D, ncols), BF16),
        name="product_theirs",
        **params_of(2 * T * D * ncols, 2 * (T * D + T * ncols + D * ncols)),
    )(idx, acts, cot, *after)


def ahead(idx_ref, axis, o):
    return lax.rem(idx_ref["cxy".index(axis)] + o, 4)


def product_for_y(acts, cot, got, idx, base, part, after=()):
    half = D // 2
    upper, lower = slice(0, half), slice(half, D)
    full, one_upper, one_lower = (2, 3, 1) if part == 0 else (0, 1, 3)
    full_lower = 1 if part == 0 else 0
    one_lower_out = 0 if part == 0 else 1

    def kernel(idx_ref, a, c_full, c_upper, c_lower, r, *rest):
        outs = rest[-2:]

        def add(product, rows, o):
            columns = pl.ds(pl.multiple_of(lax.rem(idx_ref[2] + o, NY) * TN, TN), TN)
            return (product + r[rows, columns].astype(F32)).astype(BF16)

        product = lax.dot_general(a[...], c_full[...], DN, preferred_element_type=F32)
        outs[0][upper, :] = add(product[upper], upper, full)
        outs[full_lower][lower, :] = add(product[lower], lower, full)
        product = lax.dot_general(a[:, upper], c_upper[...], DN, preferred_element_type=F32)
        outs[1][upper, :] = add(product, upper, one_upper)
        product = lax.dot_general(a[:, lower], c_lower[...], DN, preferred_element_type=F32)
        outs[one_lower_out][lower, :] = add(product, lower, one_lower)

    def columns(o):
        place = lambda j, s: (0, s[0] * (HALF // TN) + base // TN + lax.rem(s[2] + o, NY))
        return pl.BlockSpec((T, TN), place)

    return pl.pallas_call(
        kernel,
        grid_spec=pltpu.PrefetchScalarGridSpec(
            num_scalar_prefetch=1,
            grid=(1,),
            in_specs=[WHOLE]
            + [columns(o) for o in (full, one_upper, one_lower)]
            + [WHOLE]
            + [pl.BlockSpec(memory_space=pl.ANY)] * len(after),
            out_specs=[WHOLE] * 2,
        ),
        out_shape=[jax.ShapeDtypeStruct((D, TN), BF16)] * 2,
        name="product_for_y",
        **params_of(4 * T * D * TN, 2 * (T * D + 4 * T * TN + 4 * D * TN)),
    )(idx, acts, cot, cot, cot, got, *after)


def product_for_x(acts, cot, got, idx, base, ncols, after):
    tn = 2 * TN

    def kernel(idx_ref, a, c, r, _, *outs):
        acc = lax.dot_general(a[...], c[...], DN, preferred_element_type=F32) + r[...].astype(F32)
        acc = acc.astype(BF16).reshape(NZ, NX, BLK, tn)
        for me in range(NX):

            @pl.when(idx_ref[1] == me)
            def _():
                for o in range(NX):
                    for out, half in parts_of(o, NZ // 2):
                        outs[out][half] = acc[half, (me + o) % NX]

    shapes = [jax.ShapeDtypeStruct((NZ, BLK, ncols), BF16)] * 4
    return pl.pallas_call(
        kernel,
        grid_spec=pltpu.PrefetchScalarGridSpec(
            num_scalar_prefetch=1,
            grid=(ncols // tn,),
            in_specs=[
                WHOLE,
                pl.BlockSpec((T, tn), lambda j, s: (0, s[0] * (HALF // tn) + base // tn + j)),
                pl.BlockSpec((D, tn), lambda j, s: (0, j)),
                pl.BlockSpec(memory_space=pl.ANY),
            ],
            out_specs=[pl.BlockSpec(o.shape[:2] + (tn,), lambda j, s: (0, 0, j)) for o in shapes],
        ),
        out_shape=shapes,
        name="product_for_x",
        **params_of(2 * T * D * ncols, 2 * (T * D + T * ncols + 2 * D * ncols)),
    )(idx, acts, cot, got, after)


def parts_of(o, half):
    upper, lower = slice(0, half), slice(half, 2 * half)
    arrays = ((0, 0), (3, 1), (1, 2), (2, 3))[o]
    return ((arrays[0], upper), (arrays[1], lower))


def pass_on(keep, from_down, from_up):
    half = keep.shape[0] // 2

    def kernel(k, fd, fu, up, down):
        for n in range(half):
            up[n] = (k[n].astype(F32) + fd[n].astype(F32)).astype(BF16)
            down[n] = (k[half + n].astype(F32) + fu[half + n].astype(F32)).astype(BF16)

    return pl.pallas_call(
        kernel,
        in_specs=[WHOLE] * 3,
        out_specs=[WHOLE] * 2,
        out_shape=[jax.ShapeDtypeStruct((half,) + keep.shape[1:], BF16)] * 2,
        name="pass_on",
        **params_of(keep.size, 6 * keep.size),
    )(keep, from_down, from_up)


def ring(up, down, axis):
    return shift(up, axis, 4, 1), shift(down, axis, 4, 3)


def ring_end(own, keep, from_down, from_up, axis):
    up, down = pass_on(keep, from_down, from_up)
    return own, from_down, from_up, shift(up, axis, 4, 1), shift(down, axis, 4, 3)


def total_of(refs, z):
    total = refs[0][z].astype(F32)
    for r in refs[1:]:
        total = total + r[z].astype(F32)
    return total


def sum_and_cut(arrived, idx, axis):
    n = arrived[0].shape[0]

    def kernel(idx_ref, own, from_down, from_up, up, down, *outs):
        for o in range(4):
            t = ahead(idx_ref, axis, o)
            for z in range(NZ):
                if axis == "x":
                    place, rest = z * NX + t, slice(None)
                else:
                    place, rest = z, pl.ds(pl.multiple_of(t * TN, TN), TN)
                total = own[place, :, rest].astype(F32)
                if z < NZ // 2:
                    total = total + from_up[place, :, rest].astype(F32) + up[place, :, rest].astype(F32)
                else:
                    total = total + from_down[place, :, rest].astype(F32) + down[place - n // 2, :, rest].astype(F32)
                outs[o][z] = total.astype(BF16)

    return pl.pallas_call(
        kernel,
        grid_spec=pltpu.PrefetchScalarGridSpec(
            num_scalar_prefetch=1, grid=(1,), in_specs=[WHOLE] * 5, out_specs=[WHOLE] * 4
        ),
        out_shape=[jax.ShapeDtypeStruct((NZ, BLK, TN), BF16)] * 4,
        name="sum_for_" + axis,
        **params_of(4 * D * TN, 10 * D * TN),
    )(idx, *arrived)


def sum_for_z(flows):
    counts = [len(f) for f in flows]

    def kernel(*refs):
        ins, o = refs[:-1], refs[-1]
        for z in range(NZ):
            totals = [total_of(ins[: counts[0]], z), total_of(ins[counts[0] :], z)]
            for y in range(NY):
                rows = [t[h * NY * OWN + y * OWN : h * NY * OWN + (y + 1) * OWN] for t in totals for h in range(NC)]
                o[z * NY + y] = jnp.concatenate(rows, axis=0).astype(BF16)

    return pl.pallas_call(
        kernel,
        in_specs=[WHOLE] * sum(counts),
        out_specs=WHOLE,
        out_shape=jax.ShapeDtypeStruct((NZ * NY, 2 * NC * OWN, TN), BF16),
        name="sum_for_z",
        **params_of(8 * D * TN, 20 * D * TN),
    )(*flows[0], *flows[1])


def settle(flows, c):
    pieces = swap(sum_for_z(flows), ("z", "y")).astype(F32)
    pieces = jnp.sum(pieces.reshape(NZ, NY, 2, NC, OWN, TN), axis=0)
    mine, theirs = [
        lax.select_n(c == h, pieces[:, :, 1], pieces[:, :, 0]).astype(BF16) for h in (0, 1)
    ]
    got = shift(theirs, "c", NC, 1)
    halves = [lax.select_n(c == h, got, mine) for h in range(NC)]
    return jnp.concatenate([p[k, f] for p in halves for f in range(2) for k in range(NY)], axis=-1).astype(F32)


def body(acts, cotangent, master, moment, second):
    x, c, y = (lax.axis_index(a) for a in ("x", "c", "y"))
    idx = jnp.stack([c, x, y]).astype(jnp.int32)
    blocks = lambda p: p.reshape(NZ * NX, BLK, TN)
    theirs_c = product(acts, cotangent, idx, 0, FLOW_C)
    got_c = shift(theirs_c, "c", NC, 1)
    theirs_b = product(acts, cotangent, idx, FLOW_C, FLOW_B, (theirs_c,))
    got_b = shift(theirs_b, "c", NC, 1)
    up, down = product_for_y(acts, cotangent, got_c, idx, 0, 0)
    first_y = ring(blocks(up), blocks(down), "y")
    own_b, up_b, down_b, keep_b = product_for_x(acts, cotangent, got_b, idx, FLOW_C, FLOW_B, up)
    first_x = ring(up_b, down_b, "x")
    own, keep = product_for_y(acts, cotangent, got_c, idx, 0, 1, (own_b,))
    over_y = ring_end(blocks(own), blocks(keep), *first_y, "y")
    over_x = ring_end(own_b, keep_b, *first_x, "x")
    over_xy = exchange(sum_and_cut(over_x, idx, "y"), "y", 4, ORDER)
    over_yx = exchange(sum_and_cut(over_y, idx, "x"), "x", 4, ORDER)
    grad = settle((over_yx, over_xy), c)
    new_moment = 0.9 * moment + 0.1 * grad
    new_second = 0.95 * second + 0.05 * grad * grad
    corr_one = 1.0 - 0.9**10
    corr_two = 1.0 - 0.95**10
    update = new_moment / corr_one / (jnp.sqrt(new_second / corr_two) + 1e-08)
    new_master = master - 0.02 * (update + 0.1 * master)
    every = exchange([new_master.astype(BF16)] * NY, "y", NY, (1, 2, 3))
    params = jnp.concatenate([lax.select_n(lax.rem(y - k + NY, NY), *every) for k in range(NY)], axis=0)
    return (new_master, new_moment, new_second, params)


def solution(mesh):
    fine = Mesh(mesh.devices.reshape(NZ, NX, NC, NY), ("z", "x", "c", "y"))
    split = P(("z", "x", "c", "y"), None)
    return jax.shard_map(
        body,
        mesh=fine,
        in_specs=(split,) * 5,
        out_specs=(split, split, split, P(("z", "x", "c"), None)),
        check_vma=False,
    )
```
